1024 devices in a mesh: ctx: 64 (over z, x), head: 16 (over y, core).
Axes of the slice: x: 8, y: 8, z: 8, core: 2. Of those that a mesh axis runs over, the one named last changes fastest.
Arguments:
- query_nope: bfloat16 [256, 16384], P('head'), may hold values from -6 to 6
- query_rope: bfloat16 [256, 8192], P('head'), may hold values from -10 to 10
- latent_cache: bfloat16 [32768, 512], P('ctx'), may hold values from -6 to 6
- rope_keys: bfloat16 [64, 32768], P(None, 'ctx'), may hold values from -6 to 6
- absorb_keys: bfloat16 [128, 128, 512], P('head'), may hold values from -0.5 to 0.5
- expand_values: bfloat16 [128, 512, 128], P('head'), may hold values from -2.09375 to 2.09375
- block_ids: int32 [128, 2, 16], P('head'), may hold values from -1 to 255, as said below
- block_counts: int32 [128, 2], P('head'), may hold values from 8 to 16
Outputs:
- attended: bfloat16 [256, 16384], P('head')
The draws below stay inside these ranges and needn't reach their ends.
Inputs may be any that keep to these rules, and one draw needn't show every extreme that they name: `block_ids`: entries beyond block_counts are -1; the first block_counts entries are distinct blocks, none after the query block's own block 254 + q, and entry 0 is that own block.
All inputs are finite; a program needn't handle non-finite values.
Results may differ from the reference program's by a relative error of at most 0.0066.
Values may be sent and summed in bfloat16 or wider, within the bound.
A program may use at most 32 MiB of HBM per device.

```python
import math
import jax
import jax.numpy as jnp
from jax import lax

HEADS = 128
NOPE = 128
ROPE = 64
LATENT = 512
VDIM = 128
BLOCK = 128
KSEL = 16
TOKENS = 256
CTX_DEV = 512
CONTEXT = 32768


def pick_blocks(key):
    block_total = CONTEXT // BLOCK
    query_blocks = TOKENS // BLOCK
    ranks = jax.random.randint(jax.random.fold_in(key, 4101), (HEADS, query_blocks, block_total), 0, 524288)
    ranks = ranks * block_total + jnp.arange(block_total, dtype=jnp.int32)
    own_block = block_total - query_blocks + jnp.arange(query_blocks, dtype=jnp.int32)
    later = jnp.arange(block_total, dtype=jnp.int32)[None, :] >= own_block[:, None]
    ranks = jnp.where(later[None], 1073741824 + jnp.arange(block_total, dtype=jnp.int32), ranks)
    order = jnp.argsort(ranks, axis=-1)[..., :KSEL - 1].astype(jnp.int32)
    first = jnp.broadcast_to(own_block[None, :, None], (HEADS, query_blocks, 1)).astype(jnp.int32)
    chosen = jnp.concatenate([first, order], axis=-1)
    counts = jax.random.randint(jax.random.fold_in(key, 4102), (HEADS, query_blocks), KSEL // 2, KSEL + 1)
    full_at = jax.random.randint(jax.random.fold_in(key, 4103), (), 0, HEADS * query_blocks)
    flat_index = jnp.arange(HEADS * query_blocks, dtype=jnp.int32).reshape(HEADS, query_blocks)
    counts = jnp.where(flat_index == full_at, KSEL, counts).astype(jnp.int32)
    chosen = jnp.where(jnp.arange(KSEL, dtype=jnp.int32)[None, None, :] < counts[..., None], chosen, -1)
    return (chosen.astype(jnp.int32), counts)


def draw_block_ids(key, part):
    return pick_blocks(key)[0]


def draw_block_counts(key, part):
    return pick_blocks(key)[1]


def draw_query_rope(key, part):
    values = jnp.clip(jax.random.normal(jax.random.fold_in(key, 5203), (TOKENS, HEADS * ROPE), jnp.float32), -6.0, 6.0)
    return values.astype(jnp.bfloat16)


def draw_rope_keys(key, part):
    values = jnp.clip(jax.random.normal(jax.random.fold_in(key, 5205), (ROPE, CONTEXT), jnp.float32), -6.0, 6.0)
    return values.astype(jnp.bfloat16)


def level_of(own_key, extent, pieces, least, high):
    def one(axis_at, parts):
        steps = jax.random.uniform(jax.random.fold_in(jax.random.fold_in(own_key, 6), axis_at), (parts,), jnp.float32, least / len(pieces), high / len(pieces))
        return jnp.repeat(jnp.exp(steps), extent[axis_at] // parts).reshape((-1,) + (1,) * (len(extent) - axis_at - 1))

    loudness = one(*pieces[0])
    for cut in pieces[1:]:
        loudness = loudness * one(*cut)
    return loudness


def normal_values(rng, extent, deviation, most, split=(), held_as=jnp.bfloat16):
    entries = jax.random.normal(rng, extent, jnp.float32) * deviation
    if len(split) > 0:
        entries = level_of(rng, extent, split, -0.22, 0.18) * entries
    return jnp.clip(entries, min=-most, max=most).astype(held_as)


def setup_inputs(seed: int = 0) -> dict:
    arg_keys = jax.random.split(jax.random.key(seed), 9)
    query_nope = normal_values(arg_keys[0], (TOKENS, HEADS * NOPE), 1.0, 6.0, ((0, 16),))
    query_rope = draw_query_rope(jax.random.fold_in(arg_keys[8], 71), 0)
    latent_cache = normal_values(arg_keys[2], (CONTEXT, LATENT), 1.0, 6.0, ((0, 64),))
    rope_keys = draw_rope_keys(jax.random.fold_in(arg_keys[8], 71), 0)
    absorb_keys = normal_values(arg_keys[4], (HEADS, NOPE, LATENT), NOPE ** -0.5, 0.5, ((0, 16),))
    expand_values = normal_values(arg_keys[5], (HEADS, LATENT, VDIM), 0.35, 2.09375, ((0, 16),))
    block_ids = draw_block_ids(jax.random.fold_in(arg_keys[8], 71), 0)
    block_counts = draw_block_counts(jax.random.fold_in(arg_keys[8], 71), 0)
    return {"query_nope": query_nope, "query_rope": query_rope, "latent_cache": latent_cache, "rope_keys": rope_keys, "absorb_keys": absorb_keys, "expand_values": expand_values, "block_ids": block_ids, "block_counts": block_counts}


def reference(query_nope, query_rope, latent_cache, rope_keys, absorb_keys, expand_values, block_ids, block_counts):
    tokens = query_nope.shape[0]
    heads = absorb_keys.shape[0]
    nope_width = absorb_keys.shape[1]
    latent_width = absorb_keys.shape[2]
    rope_width = rope_keys.shape[0]
    value_width = expand_values.shape[2]
    context = latent_cache.shape[0]
    block_total = context // BLOCK
    query_blocks = tokens // BLOCK
    slot_count = block_ids.shape[2]
    score_scale = 1.0 / math.sqrt(nope_width + rope_width)
    key_blocks = latent_cache.reshape(block_total, BLOCK, latent_width)
    rope_blocks = rope_keys.reshape(rope_width, block_total, BLOCK).transpose(1, 0, 2)
    nope_heads = query_nope.reshape(tokens, heads, nope_width).transpose(1, 0, 2)
    rope_heads = query_rope.reshape(tokens, heads, rope_width).transpose(1, 0, 2)
    offset = context - tokens

    def one_head(head_args):
        nope_rows, rope_rows, key_proj, value_proj, head_ids, head_counts = head_args
        query_latent = jnp.dot(nope_rows, key_proj, preferred_element_type=jnp.float32).astype(jnp.bfloat16)
        value_float = value_proj.astype(jnp.float32)

        def one_block(block_args):
            block_index, row_ids, count = block_args
            start = (block_index * BLOCK).astype(jnp.int32)
            latent_rows = lax.dynamic_slice_in_dim(query_latent, start, BLOCK, 0)
            rope_part = lax.dynamic_slice_in_dim(rope_rows, start, BLOCK, 0)
            safe_ids = jnp.maximum(row_ids, 0).astype(jnp.int32)
            keys = key_blocks[safe_ids].reshape(slot_count * BLOCK, latent_width)
            rope_cols = rope_blocks[safe_ids].transpose(1, 0, 2).reshape(rope_width, slot_count * BLOCK)
            scores = jnp.dot(latent_rows, keys.T, preferred_element_type=jnp.float32)
            scores = (scores + jnp.dot(rope_part, rope_cols, preferred_element_type=jnp.float32)) * score_scale
            query_pos = offset + start + jnp.arange(BLOCK, dtype=jnp.int32)
            key_pos = (safe_ids[:, None] * BLOCK + jnp.arange(BLOCK, dtype=jnp.int32)[None, :]).reshape(-1)
            slot_live = jnp.broadcast_to((jnp.arange(slot_count, dtype=jnp.int32) < count)[:, None], (slot_count, BLOCK)).reshape(-1)
            allowed = slot_live[None, :] & (key_pos[None, :] <= query_pos[:, None])
            masked = jnp.where(allowed, scores, -1e+30).reshape(BLOCK, slot_count, BLOCK)
            slot_max = lax.optimization_barrier(jnp.max(masked, axis=2))
            slot_segment = safe_ids * BLOCK // CTX_DEV
            same = slot_segment[:, None] == slot_segment[None, :]
            segment_top = lax.optimization_barrier(jnp.max(jnp.where(same[None], slot_max[:, None, :], -1e+30), axis=2))
            row_top = lax.optimization_barrier(jnp.max(slot_max, axis=1, keepdims=True))
            segment_cols = jnp.repeat(segment_top, BLOCK, axis=1)
            weights = jnp.where(allowed, jnp.exp(scores - segment_cols), 0.0).astype(jnp.bfloat16)
            segment_scale = jnp.exp(segment_top - row_top)
            weight_float = weights.astype(jnp.float32).reshape(BLOCK, slot_count, BLOCK)
            weight_total = lax.optimization_barrier(jnp.sum(segment_scale * lax.optimization_barrier(jnp.sum(weight_float, axis=2)), axis=1, keepdims=True))
            partial_value = jnp.einsum('rsk,skl->rsl', weight_float, keys.astype(jnp.float32).reshape(slot_count, BLOCK, latent_width), precision=lax.Precision.HIGHEST)
            latent_sum = lax.optimization_barrier(jnp.sum(segment_scale[:, :, None] * partial_value, axis=1))
            result = jnp.dot(latent_sum, value_float, precision=lax.Precision.HIGHEST) / weight_total
            return result.astype(jnp.bfloat16)
        outputs = lax.map(one_block, (jnp.arange(query_blocks, dtype=jnp.int32), head_ids, head_counts))
        return outputs.reshape(tokens, value_width)
    per_head = lax.map(one_head, (nope_heads, rope_heads, absorb_keys, expand_values, block_ids, block_counts))
    return per_head.transpose(1, 0, 2).reshape(tokens, heads * value_width)
```

```python
import functools
import math

import jax
import jax.numpy as jnp
from jax import lax
from jax.experimental import pallas as pl
from jax.experimental.pallas import tpu as pltpu
from jax.sharding import PartitionSpec as P

BLOCK = 128
MESH = pl.DeviceIdType.MESH
NONE = -1e30
F32 = jnp.float32
BF16 = jnp.bfloat16


def ring_order(n):
    order = []
    for d in range(1, n // 2 + 1):
        order.append(d)
        if n - d not in order:
            order.append(n - d)
    return order


def wait_bytes(ref, sem):
    pltpu.make_async_copy(ref, ref, sem).wait()


def kernel(
    n,
    qn_hbm,
    qr_hbm,
    lat_hbm,
    rk_hbm,
    ak_hbm,
    ev_hbm,
    ids_ref,
    counts_ref,
    out_ref,
    qn,
    qr,
    lat,
    rk,
    ak,
    ev,
    rkpad,
    vext,
    bias,
    q_send,
    q_recv,
    o1_send,
    l1_send,
    o1_recv,
    l1_recv,
    o2_send,
    l2_send,
    o2_recv,
    l2_recv,
    done,
    rows_all,
    load_sem,
    qs_sem,
    qr_sem,
    s1_sem,
    r1_sem,
    s2_sem,
    r2_sem,
    s3_sem,
    r3_sem,
    s4_sem,
    r4_sem,
):
    c = lax.axis_index("ctx")
    g = lax.axis_index("head")
    z, x = c // n, lax.rem(c, n)
    y, core = g // 2, lax.rem(g, 2)
    tok = qn.shape[0]
    half = n * tok
    nope = ak.shape[1]
    rope = rk.shape[0]
    keys = lat.shape[0]
    slots = ids_ref.shape[2]
    vdim = ev.shape[2]
    pairs = n // 2
    wn, wr = 2 * nope, 2 * rope
    ring = ring_order(n)

    loads = [
        pltpu.make_async_copy(src, dst, load_sem.at[i])
        for i, (src, dst) in enumerate(
            (
                (qn_hbm, qn),
                (qr_hbm, qr),
                (lat_hbm, lat),
                (ev_hbm, ev),
                (rk_hbm, rk),
                (ak_hbm, ak),
            )
        )
    ]
    for copy in loads:
        copy.start()

    def at(pos, d):
        return lax.rem(pos + d, n)

    y_peers = [(0, 1)] + [(d, dc) for d in ring for dc in (0, 1)]
    barrier = pltpu.get_barrier_semaphore()
    for d, dc in y_peers:
        peer = 2 * at(y, d) + lax.rem(core + dc, 2)
        pl.semaphore_signal(barrier, inc=1, device_id=(c, peer), device_id_type=MESH)
    for d in ring:
        pl.semaphore_signal(barrier, inc=1, device_id=(z * n + at(x, d), g), device_id_type=MESH)
        pl.semaphore_signal(barrier, inc=1, device_id=(at(z, d) * n + x, g), device_id_type=MESH)

    loads[0].wait()
    loads[1].wait()
    for to in range(2 * n):
        for p in range(pairs):
            at_n = (to * pairs + p) * wn
            at_r = (to * pairs + p) * wr
            q_send[p, to, :, 0:wn] = qn[:, at_n : at_n + wn]
            q_send[p, to, :, wn : wn + wr] = qr[:, at_r : at_r + wr]
    first = lax.rem(x + z, n) // 2
    my_rows = pl.multiple_of(core * half + y * tok, tok)

    pl.semaphore_wait(barrier, len(y_peers) + 2 * len(ring))

    def send_pair(i, carry):
        p = lax.rem(first + i, pairs)
        for d, dc in y_peers:
            peer = 2 * at(y, d) + lax.rem(core + dc, 2)
            pltpu.make_async_remote_copy(
                src_ref=q_send.at[p, peer],
                dst_ref=q_recv.at[p, pl.ds(my_rows, tok)],
                send_sem=qs_sem,
                recv_sem=qr_sem.at[p],
                device_id=(c, peer),
                device_id_type=MESH,
            ).start()
        return carry

    lax.fori_loop(0, pairs, send_pair, 0)
    for p in range(pairs):
        q_recv[p, pl.ds(my_rows, tok)] = q_send[p, g]

    lane = lax.broadcasted_iota(jnp.int32, (1, slots), 1)
    for h in range(n):
        for q in range(2):
            ids = ids_ref[h, q : q + 1, :]
            live = lane < counts_ref[q, h]
            for b in range(keys // BLOCK):
                hit = (ids == c * (keys // BLOCK) + b) & live
                chosen = jnp.max(jnp.where(hit, 0.0, NONE), axis=1, keepdims=True)
                bias[h, q : q + 1, b * BLOCK : (b + 1) * BLOCK] = jnp.broadcast_to(chosen, (1, BLOCK))

    loads[4].wait()
    rkpad[...] = jnp.zeros_like(rkpad)
    rkpad[0, 0:rope] = rk[...]
    rkpad[1, rope : 2 * rope] = rk[...]
    loads[2].wait()
    loads[3].wait()
    vext[:, :, vdim:] = jnp.ones((n, keys, vext.shape[2] - vdim), BF16)

    def make_values(h, carry):
        vext[h, :, 0:vdim] = jnp.dot(lat[...], ev[h], preferred_element_type=F32).astype(BF16)
        return carry

    lax.fori_loop(0, n, make_values, 0)
    loads[5].wait()

    scale = 1.0 / math.sqrt(nope + rope)
    row = lax.broadcasted_iota(jnp.int32, (2 * half, 1), 0)
    in_half = lax.rem(row, half)
    token = (2 * (in_half // tok) + row // half) * tok + lax.rem(in_half, tok)
    context = keys * n * n
    query_pos = context - 2 * half + token
    late = keys // 2
    key_pos = c * keys + late + lax.broadcasted_iota(jnp.int32, (1, keys - late), 1)

    def attend(i, carry):
        p = lax.rem(first + i, pairs)
        wait_bytes(q_recv.at[p, pl.ds(0, 2 * half - tok)], qr_sem.at[p])
        for k in range(2):
            h = 2 * p + k
            query_latent = jnp.dot(
                q_recv[p, :, k * nope : (k + 1) * nope], ak[h], preferred_element_type=F32
            ).astype(BF16)
            scores = lax.dot_general(
                query_latent, lat[...], (((1,), (1,)), ((), ())), preferred_element_type=F32
            )
            scores = scores + jnp.dot(
                q_recv[p, :, wn : wn + wr], rkpad[k], preferred_element_type=F32
            )
            scores = scores * scale
            low, high = bias[h, 0:1], bias[h, 1:2]
            quarter = (half // 2, keys)
            mask = jnp.concatenate(
                [jnp.broadcast_to(v, quarter) for v in (low, high, low, high)], axis=0
            )
            scores = scores + mask
            scores = jnp.concatenate(
                [
                    scores[:, :late],
                    jnp.where(key_pos <= query_pos, scores[:, late:], NONE),
                ],
                axis=1,
            )
            top = jnp.max(scores, axis=1, keepdims=True)
            weights = jnp.exp(scores - top).astype(BF16)
            summed = jnp.dot(weights, vext[h], preferred_element_type=F32)
            total = summed[:, vdim : 2 * vdim]
            mixed = summed[:, :vdim] / total
            level = top + jnp.log(total)
            for e in range(2):
                part = slice(e * half, (e + 1) * half)
                o1_send[e, h] = mixed[part].astype(BF16)
                l1_send[e, h] = jnp.transpose(level[part, 0:BLOCK])[0:8]
                mine = x if e == 0 else z
                to = z * n + h if e == 0 else h * n + x
                slot = lax.rem(h - mine + n, n) - 1

                @pl.when(h != mine)
                def _(e=e, h=h, to=to, slot=slot):
                    pltpu.make_async_remote_copy(
                        src_ref=o1_send.at[e, h],
                        dst_ref=o1_recv.at[e, slot],
                        send_sem=s1_sem.at[e, 0],
                        recv_sem=r1_sem.at[e, 0],
                        device_id=(to, g),
                        device_id_type=MESH,
                    ).start()
                    pltpu.make_async_remote_copy(
                        src_ref=l1_send.at[e, h],
                        dst_ref=l1_recv.at[e, slot],
                        send_sem=s1_sem.at[e, 1],
                        recv_sem=r1_sem.at[e, 1],
                        device_id=(to, g),
                        device_id_type=MESH,
                    ).start()

        return carry

    lax.fori_loop(0, pairs, attend, 0)

    for e in range(2):
        mine = x if e == 0 else z
        wait_bytes(o1_recv.at[e], r1_sem.at[e, 0])
        wait_bytes(l1_recv.at[e], r1_sem.at[e, 1])
        levels = jnp.concatenate(
            [l1_send[e, mine][0:1]] + [l1_recv[e, k][0:1] for k in range(n - 1)], axis=0
        )
        top = jnp.max(levels, axis=0, keepdims=True)
        share = jnp.exp(levels - top)
        whole = jnp.sum(share, axis=0, keepdims=True)
        table = jnp.concatenate(
            [share / whole, jnp.broadcast_to(top + jnp.log(whole), (n, half))], axis=0
        )
        columns = jnp.transpose(table)
        mixed = columns[:, 0:1] * o1_send[e, mine].astype(F32)
        for k in range(n - 1):
            mixed = mixed + columns[:, k + 1 : k + 2] * o1_recv[e, k].astype(F32)
        o2_send[e] = mixed.astype(BF16)
        l2_send[e] = jnp.broadcast_to(columns[:, n : n + 1], (half, BLOCK))
        for d in ring:
            other = at(z, d) if e == 0 else at(x, d)
            to = other * n + x if e == 0 else z * n + other
            rows = pl.ds(pl.multiple_of(other * tok, tok), tok)
            pltpu.make_async_remote_copy(
                src_ref=o2_send.at[e, rows],
                dst_ref=o2_recv.at[e, d - 1],
                send_sem=s2_sem.at[e, 0],
                recv_sem=r2_sem.at[e, 0],
                device_id=(to, g),
                device_id_type=MESH,
            ).start()
            pltpu.make_async_remote_copy(
                src_ref=l2_send.at[e, rows],
                dst_ref=l2_recv.at[e, d - 1],
                send_sem=s2_sem.at[e, 1],
                recv_sem=r2_sem.at[e, 1],
                device_id=(to, g),
                device_id_type=MESH,
            ).start()

    selves = []
    for e in range(2):
        pos = z if e == 0 else x
        wait_bytes(o2_recv.at[e], r2_sem.at[e, 0])
        wait_bytes(l2_recv.at[e], r2_sem.at[e, 1])
        rows = pl.ds(pl.multiple_of(pos * tok, tok), tok)
        levels = [l2_send[e, rows]] + [l2_recv[e, k] for k in range(n - 1)]
        top = functools.reduce(jnp.maximum, levels)
        shares = [jnp.exp(level - top) for level in levels]
        mixed = shares[0] * o2_send[e, rows].astype(F32)
        whole = shares[0]
        for k in range(n - 1):
            mixed = mixed + shares[k + 1] * o2_recv[e, k].astype(F32)
            whole = whole + shares[k + 1]
        done[e] = (mixed / whole).astype(BF16)
        place = x if e == 0 else z
        peer = 2 * pos + e
        is_self = g == peer
        selves.append(is_self)
        for d in ring:
            to = at(z, d) * n + x if e == 0 else z * n + at(x, d)
            pltpu.make_async_remote_copy(
                src_ref=done.at[e],
                dst_ref=rows_all.at[place, g],
                send_sem=s3_sem.at[e],
                recv_sem=r3_sem,
                device_id=(to, peer),
                device_id_type=MESH,
            ).start()

        @pl.when(is_self)
        def _(e=e, place=place):
            pltpu.make_async_copy(done.at[e], rows_all.at[place, g], r3_sem).start()

        @pl.when(jnp.logical_not(is_self))
        def _(e=e, place=place, peer=peer):
            pltpu.make_async_remote_copy(
                src_ref=done.at[e],
                dst_ref=rows_all.at[place, g],
                send_sem=s3_sem.at[e],
                recv_sem=r3_sem,
                device_id=(c, peer),
                device_id_type=MESH,
            ).start()

    place = x * (1 - core) + z * core
    wait_bytes(rows_all.at[place], r3_sem)
    for d in ring:
        to = (z * n + at(x, d)) * (1 - core) + (at(z, d) * n + x) * core
        pltpu.make_async_remote_copy(
            src_ref=rows_all.at[place],
            dst_ref=rows_all.at[place],
            send_sem=s4_sem,
            recv_sem=r4_sem,
            device_id=(to, g),
            device_id_type=MESH,
        ).start()
    wait_bytes(rows_all.at[pl.ds(0, n - 1)], r4_sem)
    for s in range(n):
        for group in range(2 * n):
            col = (group * n + s) * vdim
            out_ref[:, col : col + vdim] = rows_all[s, group]

    wait_bytes(q_send.at[:, pl.ds(0, 2 * n - 1)], qs_sem)
    for e in range(2):
        wait_bytes(o1_recv.at[e], s1_sem.at[e, 0])
        wait_bytes(l1_recv.at[e], s1_sem.at[e, 1])
        wait_bytes(o2_recv.at[e], s2_sem.at[e, 0])
        wait_bytes(l2_recv.at[e], s2_sem.at[e, 1])

        @pl.when(selves[e])
        def _(e=e):
            wait_bytes(rows_all.at[0, pl.ds(0, n - 1)], s3_sem.at[e])

        @pl.when(jnp.logical_not(selves[e]))
        def _(e=e):
            wait_bytes(rows_all.at[0, pl.ds(0, n)], s3_sem.at[e])

    wait_bytes(rows_all.at[pl.ds(0, n - 1)], s4_sem)


def body(n, qn, qr, lat, rk, ak, ev, ids, counts):
    tok = qn.shape[0]
    half = n * tok
    nope, rope = ak.shape[1], rk.shape[0]
    keys, latent = lat.shape
    vdim = ev.shape[2]
    pairs = n // 2
    vmem = pltpu.VMEM
    dma = pltpu.SemaphoreType.DMA
    return pl.pallas_call(
        functools.partial(kernel, n),
        out_shape=jax.ShapeDtypeStruct((tok, 2 * n * n * vdim), BF16),
        in_specs=[pl.BlockSpec(memory_space=pltpu.HBM)] * 6
        + [pl.BlockSpec(memory_space=pltpu.VMEM), pl.BlockSpec(memory_space=pltpu.SMEM)],
        out_specs=pl.BlockSpec(memory_space=pltpu.VMEM),
        scratch_shapes=[
            vmem(qn.shape, BF16),
            vmem(qr.shape, BF16),
            vmem(lat.shape, BF16),
            vmem(rk.shape, BF16),
            vmem(ak.shape, BF16),
            vmem(ev.shape, BF16),
            vmem((2, 2 * rope, keys), BF16),
            vmem((n, keys, 2 * vdim), BF16),
            vmem((n, 2, keys), F32),
            vmem((pairs, 2 * n, tok, 2 * (nope + rope)), BF16),
            vmem((pairs, 2 * half, 2 * (nope + rope)), BF16),
            vmem((2, n, half, vdim), BF16),
            vmem((2, n, 8, half), F32),
            vmem((2, n - 1, half, vdim), BF16),
            vmem((2, n - 1, 8, half), F32),
            vmem((2, half, vdim), BF16),
            vmem((2, half, BLOCK), F32),
            vmem((2, n - 1, tok, vdim), BF16),
            vmem((2, n - 1, tok, BLOCK), F32),
            vmem((2, tok, vdim), BF16),
            vmem((n, 2 * n, tok, vdim), BF16),
            dma((6,)),
            dma,
            dma((pairs,)),
            dma((2, 2)),
            dma((2, 2)),
            dma((2, 2)),
            dma((2, 2)),
            dma((2,)),
            dma,
            dma,
            dma,
        ],
        compiler_params=pltpu.CompilerParams(
            collective_id=0, has_side_effects=True, vmem_limit_bytes=60 * 1024 * 1024
        ),
        cost_estimate=pl.CostEstimate(
            flops=3 * 10**9, bytes_accessed=4 * 10**6, transcendentals=10**6
        ),
    )(qn, qr, lat, rk, ak, ev, ids, counts.T)


def solution(mesh):
    n = math.isqrt(mesh.shape["ctx"])
    return jax.shard_map(
        functools.partial(body, n),
        mesh=mesh,
        in_specs=(
            P("head", None),
            P("head", None),
            P("ctx", None),
            P(None, "ctx"),
            P("head", None, None),
            P("head", None, None),
            P("head", None, None),
            P("head", None),
        ),
        out_specs=P("head", None),
        check_vma=False,
    )
```

```python
import functools
import math

import jax
import jax.numpy as jnp
from jax import lax
from jax.experimental import pallas as pl
from jax.experimental.pallas import tpu as pltpu
from jax.sharding import PartitionSpec as P

BLOCK = 128
MESH = pl.DeviceIdType.MESH
NONE = -1e30
TRY = "y"
F32 = jnp.float32
BF16 = jnp.bfloat16


def ring_order(n):
    order = []
    for d in range(1, n // 2 + 1):
        order.append(d)
        if n - d not in order:
            order.append(n - d)
    return order


def wait_bytes(ref, sem):
    pltpu.make_async_copy(ref, ref, sem).wait()


def kernel(
    n,
    qn_hbm,
    qr_hbm,
    lat_hbm,
    rk_hbm,
    ak_hbm,
    ev_hbm,
    ids_ref,
    counts_ref,
    out_ref,
    qn,
    qr,
    lat,
    rk,
    ak,
    ev,
    rkpad,
    vext,
    bias,
    q_send,
    q_recv,
    o1_send,
    l1_send,
    o1_recv,
    l1_recv,
    o2_send,
    l2_send,
    o2_recv,
    l2_recv,
    shares,
    done,
    rows_all,
    load_sem,
    qs_sem,
    qr_sem,
    fs_sem,
    fr_sem,
    ws_sem,
    s1_sem,
    r1_sem,
    s2_sem,
    r2_sem,
    s3_sem,
    r3_sem,
    s4_sem,
    r4_sem,
):
    c = lax.axis_index("ctx")
    g = lax.axis_index("head")
    z, x = c // n, lax.rem(c, n)
    y, core = g // 2, lax.rem(g, 2)
    tok = qn.shape[0]
    half = n * tok
    nope = ak.shape[1]
    rope = rk.shape[0]
    keys = lat.shape[0]
    slots = ids_ref.shape[2]
    vdim = ev.shape[2]
    pairs = n // 2
    wn, wr = 2 * nope, 2 * rope
    ring = ring_order(n)

    loads = [
        pltpu.make_async_copy(src, dst, load_sem.at[i])
        for i, (src, dst) in enumerate(
            (
                (qn_hbm, qn),
                (qr_hbm, qr),
                (lat_hbm, lat),
                (ev_hbm, ev),
                (rk_hbm, rk),
                (ak_hbm, ak),
            )
        )
    ]
    for copy in loads:
        copy.start()

    def at(pos, d):
        return lax.rem(pos + d, n)

    y_peers = [(0, 1)] + [(d, dc) for d in ring for dc in (0, 1)]
    barrier = pltpu.get_barrier_semaphore()
    for d, dc in y_peers:
        peer = 2 * at(y, d) + lax.rem(core + dc, 2)
        pl.semaphore_signal(barrier, inc=1, device_id=(c, peer), device_id_type=MESH)
    for d in ring:
        pl.semaphore_signal(barrier, inc=1, device_id=(z * n + at(x, d), g), device_id_type=MESH)
        pl.semaphore_signal(barrier, inc=1, device_id=(at(z, d) * n + x, g), device_id_type=MESH)

    loads[0].wait()
    loads[1].wait()
    for to in range(2 * n):
        for p in range(pairs):
            at_n = (to * pairs + p) * wn
            at_r = (to * pairs + p) * wr
            q_send[p, to, :, 0:wn] = qn[:, at_n : at_n + wn]
            q_send[p, to, :, wn : wn + wr] = qr[:, at_r : at_r + wr]
    if pairs >= 4:
        turn = lax.rem(x + z, 2)
        over_x, over_z = lax.rem(z, 2), 2 + lax.rem(x, 2)
        low, high = 1 - over_x, 5 - over_z
        plan = [
            ("y", low * (1 - turn) + high * turn),
            ("x", over_x),
            ("z", over_z),
            ("y", low * turn + high * (1 - turn)),
        ]
    else:
        plan = [(TRY, 0)]

    pl.semaphore_wait(barrier, len(y_peers) + 2 * len(ring))

    fetched = []
    for i, (way, p) in enumerate(plan):
        if way == "y":
            continue
        far = x if way == "x" else z
        chip = at(y, n - far)
        fetched.append((i, way, p, far))

        def fetch(dc, p=p, i=i, chip=chip):
            peer = 2 * chip + lax.rem(core + dc, 2)
            pltpu.make_async_remote_copy(
                src_ref=q_send.at[p, peer],
                dst_ref=q_recv.at[p, y, core],
                send_sem=fs_sem.at[i, dc],
                recv_sem=fr_sem.at[i],
                device_id=(c, peer),
                device_id_type=MESH,
            ).start()

        fetch(1)

        @pl.when(far != 0)
        def _(fetch=fetch):
            fetch(0)

        @pl.when(far == 0)
        def _(p=p, i=i):
            pltpu.make_async_copy(q_send.at[p, g], q_recv.at[p, y, core], fr_sem.at[i]).start()

    def send_direct(i, p):
        for d, dc in y_peers:
            peer = 2 * at(y, d) + lax.rem(core + dc, 2)
            pltpu.make_async_remote_copy(
                src_ref=q_send.at[p, peer],
                dst_ref=q_recv.at[p, y, core],
                send_sem=qs_sem.at[i],
                recv_sem=qr_sem.at[i],
                device_id=(c, peer),
                device_id_type=MESH,
            ).start()
        q_recv[p, y, core] = q_send[p, g]

    direct = [(i, p) for i, (way, p) in enumerate(plan) if way == "y"]
    for i, p in direct[:1]:
        send_direct(i, p)

    lane = lax.broadcasted_iota(jnp.int32, (1, slots), 1)
    for h in range(n):
        for q in range(2):
            ids = ids_ref[h, q : q + 1, :]
            live = lane < counts_ref[q, h]
            for b in range(keys // BLOCK):
                hit = (ids == c * (keys // BLOCK) + b) & live
                chosen = jnp.max(jnp.where(hit, 0.0, NONE), axis=1, keepdims=True)
                bias[h, q : q + 1, b * BLOCK : (b + 1) * BLOCK] = jnp.broadcast_to(chosen, (1, BLOCK))

    loads[4].wait()
    rkpad[...] = jnp.zeros_like(rkpad)
    rkpad[0, 0:rope] = rk[...]
    rkpad[1, rope : 2 * rope] = rk[...]
    for i, way, p, far in fetched:
        chip = at(y, far)
        wait_bytes(q_recv.at[p, chip], fr_sem.at[i])
        for d in ring:
            to = z * n + at(x, d) if way == "x" else at(z, d) * n + x
            pltpu.make_async_remote_copy(
                src_ref=q_recv.at[p, chip],
                dst_ref=q_recv.at[p, chip],
                send_sem=ws_sem.at[i],
                recv_sem=qr_sem.at[i],
                device_id=(to, g),
                device_id_type=MESH,
            ).start()
    for i, p in direct[1:]:
        send_direct(i, p)
    loads[2].wait()
    loads[3].wait()
    vext[:, :, vdim:] = jnp.ones((n, keys, vext.shape[2] - vdim), BF16)

    def make_values(h, carry):
        vext[h, :, 0:vdim] = jnp.dot(lat[...], ev[h], preferred_element_type=F32).astype(BF16)
        return carry

    lax.fori_loop(0, n, make_values, 0)
    loads[5].wait()

    scale = 1.0 / math.sqrt(nope + rope)
    row = lax.broadcasted_iota(jnp.int32, (2 * half, 1), 0)
    in_half = lax.rem(row, half)
    token = (2 * (in_half // tok) + row // half) * tok + lax.rem(in_half, tok)
    context = keys * n * n
    query_pos = context - 2 * half + token
    late = keys // 2
    key_pos = c * keys + late + lax.broadcasted_iota(jnp.int32, (1, keys - late), 1)

    def attend(i, carry):
        p = 0
        for j, (way, which) in enumerate(plan):
            p = jnp.where(i == j, which, p)

            @pl.when(i == j)
            def _(way=way, which=which, j=j):
                if way == "y":
                    wait_bytes(q_send.at[which, pl.ds(0, 2 * n - 1)], qr_sem.at[j])
                else:
                    wait_bytes(q_recv.at[which, pl.ds(0, n - 1)], qr_sem.at[j])

        queries = jnp.concatenate(
            [q_recv[p, :, e].reshape(half, wn + wr) for e in range(2)], axis=0
        )
        for k in range(2):
            h = 2 * p + k
            query_latent = jnp.dot(
                queries[:, k * nope : (k + 1) * nope], ak[h], preferred_element_type=F32
            ).astype(BF16)
            scores = lax.dot_general(
                query_latent, lat[...], (((1,), (1,)), ((), ())), preferred_element_type=F32
            )
            scores = scores + jnp.dot(
                queries[:, wn : wn + wr], rkpad[k], preferred_element_type=F32
            )
            scores = scores * scale
            low, high = bias[h, 0:1], bias[h, 1:2]
            quarter = (half // 2, keys)
            mask = jnp.concatenate(
                [jnp.broadcast_to(v, quarter) for v in (low, high, low, high)], axis=0
            )
            scores = scores + mask
            scores = jnp.concatenate(
                [
                    scores[:, :late],
                    jnp.where(key_pos <= query_pos, scores[:, late:], NONE),
                ],
                axis=1,
            )
            top = jnp.max(scores, axis=1, keepdims=True)
            weights = jnp.exp(scores - top).astype(BF16)
            summed = jnp.dot(weights, vext[h], preferred_element_type=F32)
            total = summed[:, vdim : 2 * vdim]
            mixed = summed[:, :vdim] / total
            level = top + jnp.log(total)
            for e in range(2):
                part = slice(e * half, (e + 1) * half)
                o1_send[e, h] = mixed[part].astype(BF16)
                l1_send[e, h] = jnp.transpose(level[part, 0:BLOCK])[0:1]
                mine = x if e == 0 else z
                to = z * n + h if e == 0 else h * n + x
                slot = lax.rem(h - mine + n, n) - 1

                @pl.when(h != mine)
                def _(e=e, h=h, to=to, slot=slot):
                    pltpu.make_async_remote_copy(
                        src_ref=o1_send.at[e, h],
                        dst_ref=o1_recv.at[e, slot],
                        send_sem=s1_sem.at[e, 0],
                        recv_sem=r1_sem.at[e, 0],
                        device_id=(to, g),
                        device_id_type=MESH,
                    ).start()
                    pltpu.make_async_remote_copy(
                        src_ref=l1_send.at[e, h],
                        dst_ref=l1_recv.at[e, slot],
                        send_sem=s1_sem.at[e, 1],
                        recv_sem=r1_sem.at[e, 1],
                        device_id=(to, g),
                        device_id_type=MESH,
                    ).start()

        return carry

    lax.fori_loop(0, pairs, attend, 0)

    for e in range(2):
        mine = x if e == 0 else z
        wait_bytes(o1_recv.at[e], r1_sem.at[e, 0])
        wait_bytes(l1_recv.at[e], r1_sem.at[e, 1])
        levels = jnp.concatenate(
            [l1_send[e, mine]] + [l1_recv[e, k] for k in range(n - 1)], axis=0
        )
        top = jnp.max(levels, axis=0, keepdims=True)
        share = jnp.exp(levels - top)
        whole = jnp.sum(share, axis=0, keepdims=True)
        columns = jnp.transpose(share / whole)
        mixed = columns[:, 0:1] * o1_send[e, mine].astype(F32)
        for k in range(n - 1):
            mixed = mixed + columns[:, k + 1 : k + 2] * o1_recv[e, k].astype(F32)
        o2_send[e] = mixed.astype(BF16)
        l2_send[e] = top + jnp.log(whole)
        for d in ring:
            other = at(z, d) if e == 0 else at(x, d)
            to = other * n + x if e == 0 else z * n + other
            rows = pl.ds(pl.multiple_of(other * tok, tok), tok)
            pltpu.make_async_remote_copy(
                src_ref=o2_send.at[e, rows],
                dst_ref=o2_recv.at[e, d - 1],
                send_sem=s2_sem.at[e, 0],
                recv_sem=r2_sem.at[e, 0],
                device_id=(to, g),
                device_id_type=MESH,
            ).start()
            pltpu.make_async_remote_copy(
                src_ref=l2_send.at[e],
                dst_ref=l2_recv.at[e, d - 1],
                send_sem=s2_sem.at[e, 1],
                recv_sem=r2_sem.at[e, 1],
                device_id=(to, g),
                device_id_type=MESH,
            ).start()

    selves = []
    for e in range(2):
        pos = z if e == 0 else x
        wait_bytes(o2_recv.at[e], r2_sem.at[e, 0])
        wait_bytes(l2_recv.at[e], r2_sem.at[e, 1])
        rows = pl.ds(pl.multiple_of(pos * tok, tok), tok)
        levels = jnp.concatenate([l2_send[e]] + [l2_recv[e, k] for k in range(n - 1)], axis=0)
        share = jnp.exp(levels - jnp.max(levels, axis=0, keepdims=True))
        shares[e] = jnp.transpose(share / jnp.sum(share, axis=0, keepdims=True))
        columns = shares[e, rows]
        mixed = columns[:, 0:1] * o2_send[e, rows].astype(F32)
        for k in range(n - 1):
            mixed = mixed + columns[:, k + 1 : k + 2] * o2_recv[e, k].astype(F32)
        done[e] = mixed.astype(BF16)
        place = x if e == 0 else z
        peer = 2 * pos + e
        is_self = g == peer
        step = lax.rem(y - pos + n, n)
        selves.append(is_self)
        for d in ring:
            to = at(z, d) * n + x if e == 0 else z * n + at(x, d)
            pltpu.make_async_remote_copy(
                src_ref=done.at[e],
                dst_ref=rows_all.at[place, g],
                send_sem=s3_sem.at[e],
                recv_sem=r3_sem.at[step],
                device_id=(to, peer),
                device_id_type=MESH,
            ).start()

        @pl.when(is_self)
        def _(e=e, place=place):
            pltpu.make_async_copy(done.at[e], rows_all.at[place, g], r3_sem.at[0]).start()

        @pl.when(jnp.logical_not(is_self))
        def _(e=e, place=place, peer=peer):
            pltpu.make_async_remote_copy(
                src_ref=done.at[e],
                dst_ref=rows_all.at[place, g],
                send_sem=s3_sem.at[e],
                recv_sem=r3_sem.at[step],
                device_id=(c, peer),
                device_id_type=MESH,
            ).start()

    place = x * (1 - core) + z * core
    for step in [0] + ring:
        both = rows_all.at[place, pl.ds(2 * at(y, step), 2)]
        wait_bytes(both, r3_sem.at[step])
        for d in ring:
            to = (z * n + at(x, d)) * (1 - core) + (at(z, d) * n + x) * core
            pltpu.make_async_remote_copy(
                src_ref=both,
                dst_ref=both,
                send_sem=s4_sem,
                recv_sem=r4_sem,
                device_id=(to, g),
                device_id_type=MESH,
            ).start()
    wait_bytes(rows_all.at[pl.ds(0, n - 1)], r4_sem)
    for s in range(n):
        for group in range(2 * n):
            col = (group * n + s) * vdim
            out_ref[:, col : col + vdim] = rows_all[s, group]

    for i, (way, p) in enumerate(plan):
        if way == "y":
            wait_bytes(q_send.at[p, pl.ds(0, 2 * n - 1)], qs_sem.at[i])
            continue
        wait_bytes(q_send.at[p, 0], fs_sem.at[i, 1])

        @pl.when((x if way == "x" else z) != 0)
        def _(p=p, i=i):
            wait_bytes(q_send.at[p, 0], fs_sem.at[i, 0])

        wait_bytes(q_recv.at[p, pl.ds(0, n - 1)], ws_sem.at[i])
    for e in range(2):
        wait_bytes(o1_recv.at[e], s1_sem.at[e, 0])
        wait_bytes(l1_recv.at[e], s1_sem.at[e, 1])
        wait_bytes(o2_recv.at[e], s2_sem.at[e, 0])
        wait_bytes(l2_recv.at[e], s2_sem.at[e, 1])

        @pl.when(selves[e])
        def _(e=e):
            wait_bytes(rows_all.at[0, pl.ds(0, n - 1)], s3_sem.at[e])

        @pl.when(jnp.logical_not(selves[e]))
        def _(e=e):
            wait_bytes(rows_all.at[0, pl.ds(0, n)], s3_sem.at[e])

    wait_bytes(rows_all.at[pl.ds(0, n - 1)], s4_sem)


def body(n, qn, qr, lat, rk, ak, ev, ids, counts):
    tok = qn.shape[0]
    half = n * tok
    nope, rope = ak.shape[1], rk.shape[0]
    keys, latent = lat.shape
    vdim = ev.shape[2]
    pairs = n // 2
    vmem = pltpu.VMEM
    dma = pltpu.SemaphoreType.DMA
    return pl.pallas_call(
        functools.partial(kernel, n),
        out_shape=jax.ShapeDtypeStruct((tok, 2 * n * n * vdim), BF16),
        in_specs=[pl.BlockSpec(memory_space=pltpu.HBM)] * 6
        + [pl.BlockSpec(memory_space=pltpu.VMEM), pl.BlockSpec(memory_space=pltpu.SMEM)],
        out_specs=pl.BlockSpec(memory_space=pltpu.VMEM),
        scratch_shapes=[
            vmem(qn.shape, BF16),
            vmem(qr.shape, BF16),
            vmem(lat.shape, BF16),
            vmem(rk.shape, BF16),
            vmem(ak.shape, BF16),
            vmem(ev.shape, BF16),
            vmem((2, 2 * rope, keys), BF16),
            vmem((n, keys, 2 * vdim), BF16),
            vmem((n, 2, keys), F32),
            vmem((pairs, 2 * n, tok, 2 * (nope + rope)), BF16),
            vmem((pairs, n, 2, tok, 2 * (nope + rope)), BF16),
            vmem((2, n, half, vdim), BF16),
            vmem((2, n, 1, half), F32),
            vmem((2, n - 1, half, vdim), BF16),
            vmem((2, n - 1, 1, half), F32),
            vmem((2, half, vdim), BF16),
            vmem((2, 1, half), F32),
            vmem((2, n - 1, tok, vdim), BF16),
            vmem((2, n - 1, 1, half), F32),
            vmem((2, half, n), F32),
            vmem((2, tok, vdim), BF16),
            vmem((n, 2 * n, tok, vdim), BF16),
            dma((6,)),
            dma((pairs,)),
            dma((pairs,)),
            dma((pairs, 2)),
            dma((pairs,)),
            dma((pairs,)),
            dma((2, 2)),
            dma((2, 2)),
            dma((2, 2)),
            dma((2, 2)),
            dma((2,)),
            dma((n,)),
            dma,
            dma,
        ],
        compiler_params=pltpu.CompilerParams(
            collective_id=0, has_side_effects=True, vmem_limit_bytes=60 * 1024 * 1024
        ),
        cost_estimate=pl.CostEstimate(
            flops=3 * 10**9, bytes_accessed=4 * 10**6, transcendentals=10**6
        ),
    )(qn, qr, lat, rk, ak, ev, ids, counts.T)


def solution(mesh):
    n = math.isqrt(mesh.shape["ctx"])
    return jax.shard_map(
        functools.partial(body, n),
        mesh=mesh,
        in_specs=(
            P("head", None),
            P("head", None),
            P("ctx", None),
            P(None, "ctx"),
            P("head", None, None),
            P("head", None, None),
            P("head", None, None),
            P("head", None),
        ),
        out_specs=P("head", None),
        check_vma=False,
    )
```

```python
import functools
import math

import jax
import jax.numpy as jnp
from jax import lax
from jax.experimental import pallas as pl
from jax.experimental.pallas import tpu as pltpu
from jax.sharding import PartitionSpec as P

BLOCK = 128
MESH = pl.DeviceIdType.MESH
NONE = -1e30
TRY = "y"
F32 = jnp.float32
BF16 = jnp.bfloat16


def ring_order(n):
    order = []
    for d in range(1, n // 2 + 1):
        order.append(d)
        if n - d not in order:
            order.append(n - d)
    return order


def wait_bytes(ref, sem):
    pltpu.make_async_copy(ref, ref, sem).wait()


def kernel(
    n,
    qn_hbm,
    qr_hbm,
    lat_hbm,
    rk_hbm,
    ak_hbm,
    ev_hbm,
    ids_hbm,
    counts_hbm,
    out_ref,
    qn,
    qr,
    lat,
    rk,
    ak,
    ev,
    ids_ref,
    counts_ref,
    rkpad,
    vext,
    bias,
    q_send,
    q_recv,
    o1_send,
    l1_send,
    o1_recv,
    l1_recv,
    o2_send,
    l2_send,
    o2_recv,
    l2_recv,
    shares,
    done,
    rows_all,
    load_sem,
    qs_sem,
    qr_sem,
    fs_sem,
    fr_sem,
    ws_sem,
    s1_sem,
    r1_sem,
    s2_sem,
    r2_sem,
    s3_sem,
    r3_sem,
    s4_sem,
    r4_sem,
):
    c = lax.axis_index("ctx")
    g = lax.axis_index("head")
    z, x = c // n, lax.rem(c, n)
    y, core = g // 2, lax.rem(g, 2)
    tok = qn.shape[0]
    half = n * tok
    nope = ak.shape[1]
    rope = rk.shape[0]
    keys = lat.shape[0]
    slots = ids_ref.shape[2]
    vdim = ev.shape[2]
    pairs = n // 2
    wn, wr = 2 * nope, 2 * rope
    ring = ring_order(n)

    loads = [
        pltpu.make_async_copy(src, dst, load_sem.at[i])
        for i, (src, dst) in enumerate(
            (
                (qn_hbm, qn),
                (qr_hbm, qr),
                (lat_hbm, lat),
                (ev_hbm, ev),
                (rk_hbm, rk),
                (ak_hbm, ak),
                (ids_hbm, ids_ref),
                (counts_hbm, counts_ref),
            )
        )
    ]
    for copy in loads:
        copy.start()

    def at(pos, d):
        return lax.rem(pos + d, n)

    y_peers = [(0, 1)] + [(d, dc) for d in ring for dc in (0, 1)]
    barrier = pltpu.get_barrier_semaphore()
    for d, dc in y_peers:
        peer = 2 * at(y, d) + lax.rem(core + dc, 2)
        pl.semaphore_signal(barrier, inc=1, device_id=(c, peer), device_id_type=MESH)
    for d in ring:
        pl.semaphore_signal(barrier, inc=1, device_id=(z * n + at(x, d), g), device_id_type=MESH)
        pl.semaphore_signal(barrier, inc=1, device_id=(at(z, d) * n + x, g), device_id_type=MESH)

    loads[0].wait()
    loads[1].wait()
    for to in range(2 * n):
        for p in range(pairs):
            at_n = (to * pairs + p) * wn
            at_r = (to * pairs + p) * wr
            q_send[p, to, :, 0:wn] = qn[:, at_n : at_n + wn]
            q_send[p, to, :, wn : wn + wr] = qr[:, at_r : at_r + wr]
    if pairs >= 4:
        turn = lax.rem(x + z, 2)
        over_x, over_z = lax.rem(z, 2), 2 + lax.rem(x, 2)
        low, high = 1 - over_x, 5 - over_z
        plan = [
            ("y", low * (1 - turn) + high * turn),
            ("x", over_x),
            ("z", over_z),
            ("y", low * turn + high * (1 - turn)),
        ]
    else:
        plan = [(TRY, 0)]

    pl.semaphore_wait(barrier, len(y_peers) + 2 * len(ring))

    fetched = []
    for i, (way, p) in enumerate(plan):
        if way == "y":
            continue
        far = x if way == "x" else z
        chip = at(y, n - far)
        fetched.append((i, way, p, far))

        def fetch(dc, p=p, i=i, chip=chip):
            peer = 2 * chip + lax.rem(core + dc, 2)
            pltpu.make_async_remote_copy(
                src_ref=q_send.at[p, peer],
                dst_ref=q_recv.at[p, y, core],
                send_sem=fs_sem.at[i, dc],
                recv_sem=fr_sem.at[i],
                device_id=(c, peer),
                device_id_type=MESH,
            ).start()

        fetch(1)

        @pl.when(far != 0)
        def _(fetch=fetch):
            fetch(0)

        @pl.when(far == 0)
        def _(p=p, i=i):
            pltpu.make_async_copy(q_send.at[p, g], q_recv.at[p, y, core], fr_sem.at[i]).start()

    def send_direct(i, p):
        for d, dc in y_peers:
            peer = 2 * at(y, d) + lax.rem(core + dc, 2)
            pltpu.make_async_remote_copy(
                src_ref=q_send.at[p, peer],
                dst_ref=q_recv.at[p, y, core],
                send_sem=qs_sem.at[i],
                recv_sem=qr_sem.at[i],
                device_id=(c, peer),
                device_id_type=MESH,
            ).start()
        q_recv[p, y, core] = q_send[p, g]

    direct = [(i, p) for i, (way, p) in enumerate(plan) if way == "y"]
    for i, p in direct[:1]:
        send_direct(i, p)

    loads[6].wait()
    loads[7].wait()
    lane = lax.broadcasted_iota(jnp.int32, (1, slots), 1)
    for h in range(n):
        for q in range(2):
            ids = ids_ref[h, q : q + 1, :]
            live = lane < counts_ref[q, h]
            for b in range(keys // BLOCK):
                hit = (ids == c * (keys // BLOCK) + b) & live
                chosen = jnp.max(jnp.where(hit, 0.0, NONE), axis=1, keepdims=True)
                bias[h, q : q + 1, b * BLOCK : (b + 1) * BLOCK] = jnp.broadcast_to(chosen, (1, BLOCK))

    loads[4].wait()
    rkpad[...] = jnp.zeros_like(rkpad)
    rkpad[0, 0:rope] = rk[...]
    rkpad[1, rope : 2 * rope] = rk[...]
    for i, way, p, far in fetched:
        chip = at(y, far)
        wait_bytes(q_recv.at[p, chip], fr_sem.at[i])
        for d in ring:
            to = z * n + at(x, d) if way == "x" else at(z, d) * n + x
            pltpu.make_async_remote_copy(
                src_ref=q_recv.at[p, chip],
                dst_ref=q_recv.at[p, chip],
                send_sem=ws_sem.at[i],
                recv_sem=qr_sem.at[i],
                device_id=(to, g),
                device_id_type=MESH,
            ).start()
    for i, p in direct[1:]:
        send_direct(i, p)
    loads[2].wait()
    loads[3].wait()
    vext[:, :, vdim:] = jnp.ones((n, keys, vext.shape[2] - vdim), BF16)

    def make_values(h, carry):
        vext[h, :, 0:vdim] = jnp.dot(lat[...], ev[h], preferred_element_type=F32).astype(BF16)
        return carry

    lax.fori_loop(0, n, make_values, 0)
    loads[5].wait()

    scale = 1.0 / math.sqrt(nope + rope)
    row = lax.broadcasted_iota(jnp.int32, (2 * half, 1), 0)
    in_half = lax.rem(row, half)
    token = (2 * (in_half // tok) + row // half) * tok + lax.rem(in_half, tok)
    context = keys * n * n
    query_pos = context - 2 * half + token
    late = keys // 2
    key_pos = c * keys + late + lax.broadcasted_iota(jnp.int32, (1, keys - late), 1)

    def attend(i, carry):
        p = 0
        for j, (way, which) in enumerate(plan):
            p = jnp.where(i == j, which, p)

            @pl.when(i == j)
            def _(way=way, which=which, j=j):
                if way == "y":
                    wait_bytes(q_send.at[which, pl.ds(0, 2 * n - 1)], qr_sem.at[j])
                else:
                    wait_bytes(q_recv.at[which, pl.ds(0, n - 1)], qr_sem.at[j])

        queries = jnp.concatenate(
            [q_recv[p, :, e].reshape(half, wn + wr) for e in range(2)], axis=0
        )
        for k in range(2):
            h = 2 * p + k
            query_latent = jnp.dot(
                queries[:, k * nope : (k + 1) * nope], ak[h], preferred_element_type=F32
            ).astype(BF16)
            scores = lax.dot_general(
                query_latent, lat[...], (((1,), (1,)), ((), ())), preferred_element_type=F32
            )
            scores = scores + jnp.dot(
                queries[:, wn : wn + wr], rkpad[k], preferred_element_type=F32
            )
            scores = scores * scale
            low, high = bias[h, 0:1], bias[h, 1:2]
            quarter = (half // 2, keys)
            mask = jnp.concatenate(
                [jnp.broadcast_to(v, quarter) for v in (low, high, low, high)], axis=0
            )
            scores = scores + mask
            scores = jnp.concatenate(
                [
                    scores[:, :late],
                    jnp.where(key_pos <= query_pos, scores[:, late:], NONE),
                ],
                axis=1,
            )
            top = jnp.max(scores, axis=1, keepdims=True)
            weights = jnp.exp(scores - top).astype(BF16)
            summed = jnp.dot(weights, vext[h], preferred_element_type=F32)
            total = summed[:, vdim : 2 * vdim]
            mixed = summed[:, :vdim] / total
            level = top + jnp.log(total)
            for e in range(2):
                part = slice(e * half, (e + 1) * half)
                o1_send[e, h] = mixed[part].astype(BF16)
                l1_send[e, h] = jnp.transpose(level[part, 0:BLOCK])[0:1]
                mine = x if e == 0 else z
                to = z * n + h if e == 0 else h * n + x
                slot = lax.rem(h - mine + n, n) - 1

                @pl.when(h != mine)
                def _(e=e, h=h, to=to, slot=slot):
                    pltpu.make_async_remote_copy(
                        src_ref=o1_send.at[e, h],
                        dst_ref=o1_recv.at[e, slot],
                        send_sem=s1_sem.at[e, 0],
                        recv_sem=r1_sem.at[e, 0],
                        device_id=(to, g),
                        device_id_type=MESH,
                    ).start()
                    pltpu.make_async_remote_copy(
                        src_ref=l1_send.at[e, h],
                        dst_ref=l1_recv.at[e, slot],
                        send_sem=s1_sem.at[e, 1],
                        recv_sem=r1_sem.at[e, 1],
                        device_id=(to, g),
                        device_id_type=MESH,
                    ).start()

        return carry

    lax.fori_loop(0, pairs, attend, 0)

    for e in range(2):
        mine = x if e == 0 else z
        wait_bytes(o1_recv.at[e], r1_sem.at[e, 0])
        wait_bytes(l1_recv.at[e], r1_sem.at[e, 1])
        levels = jnp.concatenate(
            [l1_send[e, mine]] + [l1_recv[e, k] for k in range(n - 1)], axis=0
        )
        top = jnp.max(levels, axis=0, keepdims=True)
        share = jnp.exp(levels - top)
        whole = jnp.sum(share, axis=0, keepdims=True)
        columns = jnp.transpose(share / whole)
        mixed = columns[:, 0:1] * o1_send[e, mine].astype(F32)
        for k in range(n - 1):
            mixed = mixed + columns[:, k + 1 : k + 2] * o1_recv[e, k].astype(F32)
        o2_send[e] = mixed.astype(BF16)
        l2_send[e] = top + jnp.log(whole)
        for d in ring:
            other = at(z, d) if e == 0 else at(x, d)
            to = other * n + x if e == 0 else z * n + other
            rows = pl.ds(pl.multiple_of(other * tok, tok), tok)
            pltpu.make_async_remote_copy(
                src_ref=o2_send.at[e, rows],
                dst_ref=o2_recv.at[e, d - 1],
                send_sem=s2_sem.at[e, 0],
                recv_sem=r2_sem.at[e, 0],
                device_id=(to, g),
                device_id_type=MESH,
            ).start()
            pltpu.make_async_remote_copy(
                src_ref=l2_send.at[e],
                dst_ref=l2_recv.at[e, d - 1],
                send_sem=s2_sem.at[e, 1],
                recv_sem=r2_sem.at[e, 1],
                device_id=(to, g),
                device_id_type=MESH,
            ).start()

    selves = []
    for e in range(2):
        pos = z if e == 0 else x
        wait_bytes(o2_recv.at[e], r2_sem.at[e, 0])
        wait_bytes(l2_recv.at[e], r2_sem.at[e, 1])
        rows = pl.ds(pl.multiple_of(pos * tok, tok), tok)
        levels = jnp.concatenate([l2_send[e]] + [l2_recv[e, k] for k in range(n - 1)], axis=0)
        share = jnp.exp(levels - jnp.max(levels, axis=0, keepdims=True))
        shares[e] = jnp.transpose(share / jnp.sum(share, axis=0, keepdims=True))
        columns = shares[e, rows]
        mixed = columns[:, 0:1] * o2_send[e, rows].astype(F32)
        for k in range(n - 1):
            mixed = mixed + columns[:, k + 1 : k + 2] * o2_recv[e, k].astype(F32)
        done[e] = mixed.astype(BF16)
        place = x if e == 0 else z
        peer = 2 * pos + e
        is_self = g == peer
        step = lax.rem(y - pos + n, n)
        selves.append(is_self)
        for hop, shift in enumerate((0, n // 2)):
            for d in [0] * hop + ring:
                to = at(z, d) * n + at(x, shift) if e == 0 else at(z, shift) * n + at(x, d)
                pltpu.make_async_remote_copy(
                    src_ref=done.at[e],
                    dst_ref=rows_all.at[place, g],
                    send_sem=s3_sem.at[e],
                    recv_sem=r3_sem.at[hop, step],
                    device_id=(to, peer),
                    device_id_type=MESH,
                ).start()

        @pl.when(is_self)
        def _(e=e, place=place):
            pltpu.make_async_copy(done.at[e], rows_all.at[place, g], r3_sem.at[0, 0]).start()

        @pl.when(jnp.logical_not(is_self))
        def _(e=e, place=place, peer=peer):
            pltpu.make_async_remote_copy(
                src_ref=done.at[e],
                dst_ref=rows_all.at[place, g],
                send_sem=s3_sem.at[e],
                recv_sem=r3_sem.at[0, step],
                device_id=(c, peer),
                device_id_type=MESH,
            ).start()

    place = x * (1 - core) + z * core
    near = [d for d in ring if min(d, n - d) <= n // 4]
    nearest = [d for d in ring if min(d, n - d) < n // 4]
    for hop, reach in ((0, near), (1, nearest)):
        held = at(place, hop * (n // 2))
        for step in [0] + ring:
            both = rows_all.at[held, pl.ds(2 * at(y, step), 2)]
            wait_bytes(both, r3_sem.at[hop, step])
            for d in reach:
                to = (z * n + at(x, d)) * (1 - core) + (at(z, d) * n + x) * core
                pltpu.make_async_remote_copy(
                    src_ref=both,
                    dst_ref=both,
                    send_sem=s4_sem,
                    recv_sem=r4_sem.at[(hop * (n // 2) - d) % n],
                    device_id=(to, g),
                    device_id_type=MESH,
                ).start()
    for off in [0, n // 2] + [d for d in ring if d != n // 2]:
        held = at(place, off)
        if off % (n // 2):
            wait_bytes(rows_all.at[held], r4_sem.at[off])
        for group in range(2 * n):
            col = pl.multiple_of((group * n + held) * vdim, vdim)
            out_ref[:, pl.ds(col, vdim)] = rows_all[held, group]

    for i, (way, p) in enumerate(plan):
        if way == "y":
            wait_bytes(q_send.at[p, pl.ds(0, 2 * n - 1)], qs_sem.at[i])
            continue
        wait_bytes(q_send.at[p, 0], fs_sem.at[i, 1])

        @pl.when((x if way == "x" else z) != 0)
        def _(p=p, i=i):
            wait_bytes(q_send.at[p, 0], fs_sem.at[i, 0])

        wait_bytes(q_recv.at[p, pl.ds(0, n - 1)], ws_sem.at[i])
    for e in range(2):
        wait_bytes(o1_recv.at[e], s1_sem.at[e, 0])
        wait_bytes(l1_recv.at[e], s1_sem.at[e, 1])
        wait_bytes(o2_recv.at[e], s2_sem.at[e, 0])
        wait_bytes(l2_recv.at[e], s2_sem.at[e, 1])

        @pl.when(selves[e])
        def _(e=e):
            wait_bytes(rows_all.at[0, pl.ds(0, 2 * n - 1)], s3_sem.at[e])

        @pl.when(jnp.logical_not(selves[e]))
        def _(e=e):
            wait_bytes(rows_all.at[0], s3_sem.at[e])

    if near:
        wait_bytes(rows_all.at[pl.ds(0, len(near) + len(nearest))], s4_sem)


def body(n, qn, qr, lat, rk, ak, ev, ids, counts):
    tok = qn.shape[0]
    half = n * tok
    nope, rope = ak.shape[1], rk.shape[0]
    keys, latent = lat.shape
    vdim = ev.shape[2]
    pairs = n // 2
    vmem = pltpu.VMEM
    dma = pltpu.SemaphoreType.DMA
    return pl.pallas_call(
        functools.partial(kernel, n),
        out_shape=pltpu.VMEM((tok, 2 * n * n * vdim), BF16),
        in_specs=[pl.BlockSpec(memory_space=pltpu.HBM)] * 8,
        out_specs=pl.BlockSpec(memory_space=pltpu.VMEM),
        scratch_shapes=[
            vmem(qn.shape, BF16),
            vmem(qr.shape, BF16),
            vmem(lat.shape, BF16),
            vmem(rk.shape, BF16),
            vmem(ak.shape, BF16),
            vmem(ev.shape, BF16),
            vmem(ids.shape, jnp.int32),
            pltpu.SMEM(counts.shape[::-1], jnp.int32),
            vmem((2, 2 * rope, keys), BF16),
            vmem((n, keys, 2 * vdim), BF16),
            vmem((n, 2, keys), F32),
            vmem((pairs, 2 * n, tok, 2 * (nope + rope)), BF16),
            vmem((pairs, n, 2, tok, 2 * (nope + rope)), BF16),
            vmem((2, n, half, vdim), BF16),
            vmem((2, n, 1, half), F32),
            vmem((2, n - 1, half, vdim), BF16),
            vmem((2, n - 1, 1, half), F32),
            vmem((2, half, vdim), BF16),
            vmem((2, 1, half), F32),
            vmem((2, n - 1, tok, vdim), BF16),
            vmem((2, n - 1, 1, half), F32),
            vmem((2, half, n), F32),
            vmem((2, tok, vdim), BF16),
            vmem((n, 2 * n, tok, vdim), BF16),
            dma((8,)),
            dma((pairs,)),
            dma((pairs,)),
            dma((pairs, 2)),
            dma((pairs,)),
            dma((pairs,)),
            dma((2, 2)),
            dma((2, 2)),
            dma((2, 2)),
            dma((2, 2)),
            dma((2,)),
            dma((2, n)),
            dma,
            dma((n,)),
        ],
        compiler_params=pltpu.CompilerParams(
            collective_id=0, has_side_effects=True, vmem_limit_bytes=60 * 1024 * 1024
        ),
        cost_estimate=pl.CostEstimate(
            flops=3 * 10**9, bytes_accessed=4 * 10**6, transcendentals=10**6
        ),
    )(qn, qr, lat, rk, ak, ev, ids, counts.T)


def solution(mesh):
    n = math.isqrt(mesh.shape["ctx"])
    return jax.shard_map(
        functools.partial(body, n),
        mesh=mesh,
        in_specs=(
            P("head", None),
            P("head", None),
            P("ctx", None),
            P(None, "ctx"),
            P("head", None, None),
            P("head", None, None),
            P("head", None, None),
            P("head", None),
        ),
        out_specs=P("head", None),
        check_vma=False,
    )
```

```python
import functools
import math

import jax
import jax.numpy as jnp
from jax import lax
from jax.experimental import pallas as pl
from jax.experimental.pallas import tpu as pltpu
from jax.sharding import PartitionSpec as P

BLOCK = 128
MESH = pl.DeviceIdType.MESH
NONE = -1e30
TRY = "y"
F32 = jnp.float32
BF16 = jnp.bfloat16


def ring_order(n):
    order = []
    for d in range(1, n // 2 + 1):
        order.append(d)
        if n - d not in order:
            order.append(n - d)
    return order


def wait_bytes(ref, sem):
    pltpu.make_async_copy(ref, ref, sem).wait()


def kernel(
    n,
    qn_hbm,
    qr_hbm,
    lat_hbm,
    rk_hbm,
    ak_hbm,
    ev_hbm,
    ids_hbm,
    counts_hbm,
    out_ref,
    qn,
    qr,
    lat,
    rk,
    ak,
    ev,
    ids_ref,
    counts_ref,
    rkpad,
    vext,
    bias,
    q_send,
    q_recv,
    o1_send,
    l1_send,
    o1_recv,
    l1_recv,
    o2_send,
    l2_send,
    o2_recv,
    l2_recv,
    shares,
    done,
    rows_all,
    load_sem,
    qs_sem,
    qr_sem,
    fs_sem,
    fr_sem,
    ws_sem,
    s1_sem,
    r1_sem,
    s2_sem,
    r2_sem,
    s3_sem,
    r3_sem,
    s4_sem,
    r4_sem,
):
    c = lax.axis_index("ctx")
    g = lax.axis_index("head")
    z, x = c // n, lax.rem(c, n)
    y, core = g // 2, lax.rem(g, 2)
    tok = qn.shape[0]
    half = n * tok
    nope = ak.shape[1]
    rope = rk.shape[0]
    keys = lat.shape[0]
    slots = ids_ref.shape[2]
    vdim = ev.shape[2]
    pairs = n // 2
    wn, wr = 2 * nope, 2 * rope
    ring = ring_order(n)
    near = [d for d in ring if min(d, n - d) <= n // 4]
    nearest = [d for d in ring if min(d, n - d) < n // 4]

    loads = [
        pltpu.make_async_copy(src, dst, load_sem.at[i])
        for i, (src, dst) in enumerate(
            (
                (qn_hbm, qn),
                (qr_hbm, qr),
                (lat_hbm, lat),
                (ev_hbm, ev),
                (rk_hbm, rk),
                (ak_hbm, ak),
                (ids_hbm, ids_ref),
                (counts_hbm, counts_ref),
            )
        )
    ]
    for copy in loads:
        copy.start()

    def at(pos, d):
        return lax.rem(pos + d, n)

    y_peers = [(0, 1)] + [(d, dc) for d in ring for dc in (0, 1)]
    barrier = pltpu.get_barrier_semaphore()
    for d, dc in y_peers:
        peer = 2 * at(y, d) + lax.rem(core + dc, 2)
        pl.semaphore_signal(barrier, inc=1, device_id=(c, peer), device_id_type=MESH)
    for d in ring:
        pl.semaphore_signal(barrier, inc=1, device_id=(z * n + at(x, d), g), device_id_type=MESH)
        pl.semaphore_signal(barrier, inc=1, device_id=(at(z, d) * n + x, g), device_id_type=MESH)

    loads[0].wait()
    loads[1].wait()
    for to in range(2 * n):
        for p in range(pairs):
            at_n = (to * pairs + p) * wn
            at_r = (to * pairs + p) * wr
            q_send[p, to, :, 0:wn] = qn[:, at_n : at_n + wn]
            q_send[p, to, :, wn : wn + wr] = qr[:, at_r : at_r + wr]
    if pairs >= 4:
        turn = lax.rem(x + z, 2)
        over_x, over_z = lax.rem(z, 2), 2 + lax.rem(x, 2)
        low, high = 1 - over_x, 5 - over_z
        plan = [
            ("y", low * (1 - turn) + high * turn),
            ("x", over_x),
            ("z", over_z),
            ("y", low * turn + high * (1 - turn)),
        ]
    else:
        plan = [(TRY, 0)]

    pl.semaphore_wait(barrier, len(y_peers) + 2 * len(ring))

    fetched = []
    for i, (way, p) in enumerate(plan):
        if way == "y":
            continue
        far = x if way == "x" else z
        fetched.append((i, way, p, far))
        for hop in range(2):
            chip = at(y, 2 * n - far - hop * (n // 2))

            def fetch(dc, p=p, i=i, hop=hop, chip=chip):
                peer = 2 * chip + lax.rem(core + dc, 2)
                pltpu.make_async_remote_copy(
                    src_ref=q_send.at[p, peer],
                    dst_ref=q_recv.at[p, y, core],
                    send_sem=fs_sem.at[i, hop, dc],
                    recv_sem=fr_sem.at[i, hop],
                    device_id=(c, peer),
                    device_id_type=MESH,
                ).start()

            fetch(1)

            @pl.when(far != hop * (n // 2))
            def _(fetch=fetch):
                fetch(0)

            @pl.when(far == hop * (n // 2))
            def _(p=p, i=i, hop=hop):
                pltpu.make_async_copy(q_send.at[p, g], q_recv.at[p, y, core], fr_sem.at[i, hop]).start()

    def send_direct(i, p):
        for d, dc in y_peers:
            peer = 2 * at(y, d) + lax.rem(core + dc, 2)
            pltpu.make_async_remote_copy(
                src_ref=q_send.at[p, peer],
                dst_ref=q_recv.at[p, y, core],
                send_sem=qs_sem.at[i],
                recv_sem=qr_sem.at[i],
                device_id=(c, peer),
                device_id_type=MESH,
            ).start()
        q_recv[p, y, core] = q_send[p, g]

    direct = [(i, p) for i, (way, p) in enumerate(plan) if way == "y"]
    for i, p in direct[:1]:
        send_direct(i, p)

    loads[6].wait()
    loads[7].wait()
    lane = lax.broadcasted_iota(jnp.int32, (1, slots), 1)
    for h in range(n):
        for q in range(2):
            ids = ids_ref[h, q : q + 1, :]
            live = lane < counts_ref[q, h]
            for b in range(keys // BLOCK):
                hit = (ids == c * (keys // BLOCK) + b) & live
                chosen = jnp.max(jnp.where(hit, 0.0, NONE), axis=1, keepdims=True)
                bias[h, q : q + 1, b * BLOCK : (b + 1) * BLOCK] = jnp.broadcast_to(chosen, (1, BLOCK))

    loads[4].wait()
    rkpad[...] = jnp.zeros_like(rkpad)
    rkpad[0, 0:rope] = rk[...]
    rkpad[1, rope : 2 * rope] = rk[...]
    for i, way, p, far in fetched:
        for hop, reach in ((0, near), (1, nearest)):
            chip = at(y, far + hop * (n // 2))
            wait_bytes(q_recv.at[p, chip], fr_sem.at[i, hop])
            for d in reach:
                to = z * n + at(x, d) if way == "x" else at(z, d) * n + x
                pltpu.make_async_remote_copy(
                    src_ref=q_recv.at[p, chip],
                    dst_ref=q_recv.at[p, chip],
                    send_sem=ws_sem.at[i],
                    recv_sem=qr_sem.at[i],
                    device_id=(to, g),
                    device_id_type=MESH,
                ).start()
    for i, p in direct[1:]:
        send_direct(i, p)
    loads[2].wait()
    loads[3].wait()
    vext[:, :, vdim:] = jnp.ones((n, keys, vext.shape[2] - vdim), BF16)

    def make_values(h, carry):
        vext[h, :, 0:vdim] = jnp.dot(lat[...], ev[h], preferred_element_type=F32).astype(BF16)
        return carry

    lax.fori_loop(0, n, make_values, 0)
    loads[5].wait()

    scale = 1.0 / math.sqrt(nope + rope)
    row = lax.broadcasted_iota(jnp.int32, (2 * half, 1), 0)
    in_half = lax.rem(row, half)
    token = (2 * (in_half // tok) + row // half) * tok + lax.rem(in_half, tok)
    context = keys * n * n
    query_pos = context - 2 * half + token
    late = keys // 2
    key_pos = c * keys + late + lax.broadcasted_iota(jnp.int32, (1, keys - late), 1)

    def attend(i, carry):
        p = 0
        for j, (way, which) in enumerate(plan):
            p = jnp.where(i == j, which, p)

            @pl.when(i == j)
            def _(way=way, which=which, j=j):
                if way == "y":
                    wait_bytes(q_send.at[which, pl.ds(0, 2 * n - 1)], qr_sem.at[j])
                elif near:
                    wait_bytes(q_recv.at[which, pl.ds(0, n - 2)], qr_sem.at[j])

        queries = jnp.concatenate(
            [q_recv[p, :, e].reshape(half, wn + wr) for e in range(2)], axis=0
        )
        for k in range(2):
            h = 2 * p + k
            query_latent = jnp.dot(
                queries[:, k * nope : (k + 1) * nope], ak[h], preferred_element_type=F32
            ).astype(BF16)
            scores = lax.dot_general(
                query_latent, lat[...], (((1,), (1,)), ((), ())), preferred_element_type=F32
            )
            scores = scores + jnp.dot(
                queries[:, wn : wn + wr], rkpad[k], preferred_element_type=F32
            )
            scores = scores * scale
            low, high = bias[h, 0:1], bias[h, 1:2]
            quarter = (half // 2, keys)
            mask = jnp.concatenate(
                [jnp.broadcast_to(v, quarter) for v in (low, high, low, high)], axis=0
            )
            scores = scores + mask
            scores = jnp.concatenate(
                [
                    scores[:, :late],
                    jnp.where(key_pos <= query_pos, scores[:, late:], NONE),
                ],
                axis=1,
            )
            top = jnp.max(scores, axis=1, keepdims=True)
            weights = jnp.exp(scores - top).astype(BF16)
            summed = jnp.dot(weights, vext[h], preferred_element_type=F32)
            total = summed[:, vdim : 2 * vdim]
            mixed = summed[:, :vdim] / total
            level = top + jnp.log(total)
            for e in range(2):
                part = slice(e * half, (e + 1) * half)
                o1_send[e, h] = mixed[part].astype(BF16)
                l1_send[e, h] = jnp.transpose(level[part, 0:BLOCK])[0:1]
                mine = x if e == 0 else z
                to = z * n + h if e == 0 else h * n + x
                slot = lax.rem(h - mine + n, n) - 1

                @pl.when(h != mine)
                def _(e=e, h=h, to=to, slot=slot):
                    pltpu.make_async_remote_copy(
                        src_ref=o1_send.at[e, h],
                        dst_ref=o1_recv.at[e, slot],
                        send_sem=s1_sem.at[e, 0],
                        recv_sem=r1_sem.at[e, 0],
                        device_id=(to, g),
                        device_id_type=MESH,
                    ).start()
                    pltpu.make_async_remote_copy(
                        src_ref=l1_send.at[e, h],
                        dst_ref=l1_recv.at[e, slot],
                        send_sem=s1_sem.at[e, 1],
                        recv_sem=r1_sem.at[e, 1],
                        device_id=(to, g),
                        device_id_type=MESH,
                    ).start()

        return carry

    lax.fori_loop(0, pairs, attend, 0)

    for e in range(2):
        mine = x if e == 0 else z
        wait_bytes(o1_recv.at[e], r1_sem.at[e, 0])
        wait_bytes(l1_recv.at[e], r1_sem.at[e, 1])
        levels = jnp.concatenate(
            [l1_send[e, mine]] + [l1_recv[e, k] for k in range(n - 1)], axis=0
        )
        top = jnp.max(levels, axis=0, keepdims=True)
        share = jnp.exp(levels - top)
        whole = jnp.sum(share, axis=0, keepdims=True)
        columns = jnp.transpose(share / whole)
        mixed = columns[:, 0:1] * o1_send[e, mine].astype(F32)
        for k in range(n - 1):
            mixed = mixed + columns[:, k + 1 : k + 2] * o1_recv[e, k].astype(F32)
        o2_send[e] = mixed.astype(BF16)
        l2_send[e] = top + jnp.log(whole)
        for d in ring:
            other = at(z, d) if e == 0 else at(x, d)
            to = other * n + x if e == 0 else z * n + other
            rows = pl.ds(pl.multiple_of(other * tok, tok), tok)
            pltpu.make_async_remote_copy(
                src_ref=o2_send.at[e, rows],
                dst_ref=o2_recv.at[e, d - 1],
                send_sem=s2_sem.at[e, 0],
                recv_sem=r2_sem.at[e, 0],
                device_id=(to, g),
                device_id_type=MESH,
            ).start()
            pltpu.make_async_remote_copy(
                src_ref=l2_send.at[e],
                dst_ref=l2_recv.at[e, d - 1],
                send_sem=s2_sem.at[e, 1],
                recv_sem=r2_sem.at[e, 1],
                device_id=(to, g),
                device_id_type=MESH,
            ).start()

    selves = []
    for e in range(2):
        pos = z if e == 0 else x
        wait_bytes(o2_recv.at[e], r2_sem.at[e, 0])
        wait_bytes(l2_recv.at[e], r2_sem.at[e, 1])
        rows = pl.ds(pl.multiple_of(pos * tok, tok), tok)
        levels = jnp.concatenate([l2_send[e]] + [l2_recv[e, k] for k in range(n - 1)], axis=0)
        share = jnp.exp(levels - jnp.max(levels, axis=0, keepdims=True))
        shares[e] = jnp.transpose(share / jnp.sum(share, axis=0, keepdims=True))
        columns = shares[e, rows]
        mixed = columns[:, 0:1] * o2_send[e, rows].astype(F32)
        for k in range(n - 1):
            mixed = mixed + columns[:, k + 1 : k + 2] * o2_recv[e, k].astype(F32)
        done[e] = mixed.astype(BF16)
        place = x if e == 0 else z
        peer = 2 * pos + e
        is_self = g == peer
        step = lax.rem(y - pos + n, n)
        selves.append(is_self)
        for hop, shift in enumerate((0, n // 2)):
            for d in [0] * hop + ring:
                to = at(z, d) * n + at(x, shift) if e == 0 else at(z, shift) * n + at(x, d)
                pltpu.make_async_remote_copy(
                    src_ref=done.at[e],
                    dst_ref=rows_all.at[place, g],
                    send_sem=s3_sem.at[e],
                    recv_sem=r3_sem.at[hop, step],
                    device_id=(to, peer),
                    device_id_type=MESH,
                ).start()

        @pl.when(is_self)
        def _(e=e, place=place):
            pltpu.make_async_copy(done.at[e], rows_all.at[place, g], r3_sem.at[0, 0]).start()

        @pl.when(jnp.logical_not(is_self))
        def _(e=e, place=place, peer=peer):
            pltpu.make_async_remote_copy(
                src_ref=done.at[e],
                dst_ref=rows_all.at[place, g],
                send_sem=s3_sem.at[e],
                recv_sem=r3_sem.at[0, step],
                device_id=(c, peer),
                device_id_type=MESH,
            ).start()

    place = x * (1 - core) + z * core
    for hop, reach in ((0, near), (1, nearest)):
        held = at(place, hop * (n // 2))
        for step in [0] + ring:
            both = rows_all.at[held, pl.ds(2 * at(y, step), 2)]
            wait_bytes(both, r3_sem.at[hop, step])
            for d in reach:
                to = (z * n + at(x, d)) * (1 - core) + (at(z, d) * n + x) * core
                pltpu.make_async_remote_copy(
                    src_ref=both,
                    dst_ref=both,
                    send_sem=s4_sem,
                    recv_sem=r4_sem.at[(hop * (n // 2) - d) % n],
                    device_id=(to, g),
                    device_id_type=MESH,
                ).start()
    for off in [0, n // 2] + [d for d in ring if d != n // 2]:
        held = at(place, off)
        if off % (n // 2):
            wait_bytes(rows_all.at[held], r4_sem.at[off])
        for group in range(2 * n):
            col = pl.multiple_of((group * n + held) * vdim, vdim)
            out_ref[:, pl.ds(col, vdim)] = rows_all[held, group]

    for i, (way, p) in enumerate(plan):
        if way == "y":
            wait_bytes(q_send.at[p, pl.ds(0, 2 * n - 1)], qs_sem.at[i])
            continue
        for hop in range(2):
            wait_bytes(q_send.at[p, 0], fs_sem.at[i, hop, 1])

            @pl.when((x if way == "x" else z) != hop * (n // 2))
            def _(p=p, i=i, hop=hop):
                wait_bytes(q_send.at[p, 0], fs_sem.at[i, hop, 0])

        if near:
            wait_bytes(q_recv.at[p, pl.ds(0, n - 2)], ws_sem.at[i])
    for e in range(2):
        wait_bytes(o1_recv.at[e], s1_sem.at[e, 0])
        wait_bytes(l1_recv.at[e], s1_sem.at[e, 1])
        wait_bytes(o2_recv.at[e], s2_sem.at[e, 0])
        wait_bytes(l2_recv.at[e], s2_sem.at[e, 1])

        @pl.when(selves[e])
        def _(e=e):
            wait_bytes(rows_all.at[0, pl.ds(0, 2 * n - 1)], s3_sem.at[e])

        @pl.when(jnp.logical_not(selves[e]))
        def _(e=e):
            wait_bytes(rows_all.at[0], s3_sem.at[e])

    if near:
        wait_bytes(rows_all.at[pl.ds(0, len(near) + len(nearest))], s4_sem)


def body(n, qn, qr, lat, rk, ak, ev, ids, counts):
    tok = qn.shape[0]
    half = n * tok
    nope, rope = ak.shape[1], rk.shape[0]
    keys, latent = lat.shape
    vdim = ev.shape[2]
    pairs = n // 2
    vmem = pltpu.VMEM
    dma = pltpu.SemaphoreType.DMA
    return pl.pallas_call(
        functools.partial(kernel, n),
        out_shape=pltpu.VMEM((tok, 2 * n * n * vdim), BF16),
        in_specs=[pl.BlockSpec(memory_space=pltpu.HBM)] * 8,
        out_specs=pl.BlockSpec(memory_space=pltpu.VMEM),
        scratch_shapes=[
            vmem(qn.shape, BF16),
            vmem(qr.shape, BF16),
            vmem(lat.shape, BF16),
            vmem(rk.shape, BF16),
            vmem(ak.shape, BF16),
            vmem(ev.shape, BF16),
            vmem(ids.shape, jnp.int32),
            pltpu.SMEM(counts.shape[::-1], jnp.int32),
            vmem((2, 2 * rope, keys), BF16),
            vmem((n, keys, 2 * vdim), BF16),
            vmem((n, 2, keys), F32),
            vmem((pairs, 2 * n, tok, 2 * (nope + rope)), BF16),
            vmem((pairs, n, 2, tok, 2 * (nope + rope)), BF16),
            vmem((2, n, half, vdim), BF16),
            vmem((2, n, 1, half), F32),
            vmem((2, n - 1, half, vdim), BF16),
            vmem((2, n - 1, 1, half), F32),
            vmem((2, half, vdim), BF16),
            vmem((2, 1, half), F32),
            vmem((2, n - 1, tok, vdim), BF16),
            vmem((2, n - 1, 1, half), F32),
            vmem((2, half, n), F32),
            vmem((2, tok, vdim), BF16),
            vmem((n, 2 * n, tok, vdim), BF16),
            dma((8,)),
            dma((pairs,)),
            dma((pairs,)),
            dma((pairs, 2, 2)),
            dma((pairs, 2)),
            dma((pairs,)),
            dma((2, 2)),
            dma((2, 2)),
            dma((2, 2)),
            dma((2, 2)),
            dma((2,)),
            dma((2, n)),
            dma,
            dma((n,)),
        ],
        compiler_params=pltpu.CompilerParams(
            collective_id=0, has_side_effects=True, vmem_limit_bytes=60 * 1024 * 1024
        ),
        cost_estimate=pl.CostEstimate(
            flops=3 * 10**9, bytes_accessed=4 * 10**6, transcendentals=10**6
        ),
    )(qn, qr, lat, rk, ak, ev, ids, counts.T)


def solution(mesh):
    n = math.isqrt(mesh.shape["ctx"])
    return jax.shard_map(
        functools.partial(body, n),
        mesh=mesh,
        in_specs=(
            P("head", None),
            P("head", None),
            P("ctx", None),
            P(None, "ctx"),
            P("head", None, None),
            P("head", None, None),
            P("head", None, None),
            P("head", None),
        ),
        out_specs=P("head", None),
        check_vma=False,
    )
```

```python
import functools
import math

import jax
import jax.numpy as jnp
from jax import lax
from jax.experimental import pallas as pl
from jax.experimental.pallas import tpu as pltpu
from jax.sharding import PartitionSpec as P

BLOCK = 128
MESH = pl.DeviceIdType.MESH
NONE = -1e30
TRY = "y"
F32 = jnp.float32
BF16 = jnp.bfloat16


def ring_order(n):
    order = []
    for d in range(1, n // 2 + 1):
        order.append(d)
        if n - d not in order:
            order.append(n - d)
    return order


def wait_bytes(ref, sem):
    pltpu.make_async_copy(ref, ref, sem).wait()


def kernel(
    n,
    qn_hbm,
    qr_hbm,
    lat_hbm,
    rk_hbm,
    ak_hbm,
    ev_hbm,
    ids_hbm,
    counts_hbm,
    out_ref,
    qn,
    qr,
    lat,
    rk,
    ak,
    ev,
    ids_ref,
    counts_ref,
    rkpad,
    vext,
    bias,
    q_send,
    q_recv,
    o1_send,
    l1_send,
    o1_recv,
    l1_recv,
    o2_send,
    l2_send,
    o2_recv,
    l2_recv,
    shares,
    done,
    rows_all,
    load_sem,
    qs_sem,
    qr_sem,
    fs_sem,
    fr_sem,
    ws_sem,
    s1_sem,
    r1_sem,
    s2_sem,
    r2_sem,
    s3_sem,
    r3_sem,
    s4_sem,
    r4_sem,
):
    c = lax.axis_index("ctx")
    g = lax.axis_index("head")
    z, x = c // n, lax.rem(c, n)
    y, core = g // 2, lax.rem(g, 2)
    tok = qn.shape[0]
    half = n * tok
    nope = ak.shape[1]
    rope = rk.shape[0]
    keys = lat.shape[0]
    slots = ids_ref.shape[2]
    vdim = ev.shape[2]
    pairs = n // 2
    wn, wr = 2 * nope, 2 * rope
    ring = ring_order(n)
    near = [d for d in ring if min(d, n - d) <= n // 4]
    nearest = [d for d in ring if min(d, n - d) < n // 4]

    loads = [
        pltpu.make_async_copy(src, dst, load_sem.at[i])
        for i, (src, dst) in enumerate(
            (
                (qn_hbm, qn),
                (qr_hbm, qr),
                (lat_hbm, lat),
                (ev_hbm, ev),
                (rk_hbm, rk),
                (ak_hbm, ak),
                (ids_hbm, ids_ref),
                (counts_hbm, counts_ref),
            )
        )
    ]
    for copy in loads:
        copy.start()

    def at(pos, d):
        return lax.rem(pos + d, n)

    y_peers = [(0, 1)] + [(d, dc) for d in ring for dc in (0, 1)]
    barrier = pltpu.get_barrier_semaphore()
    for d, dc in y_peers:
        peer = 2 * at(y, d) + lax.rem(core + dc, 2)
        pl.semaphore_signal(barrier, inc=1, device_id=(c, peer), device_id_type=MESH)
    for d in ring:
        pl.semaphore_signal(barrier, inc=1, device_id=(z * n + at(x, d), g), device_id_type=MESH)
        pl.semaphore_signal(barrier, inc=1, device_id=(at(z, d) * n + x, g), device_id_type=MESH)

    loads[0].wait()
    loads[1].wait()
    for to in range(2 * n):
        for p in range(pairs):
            at_n = (to * pairs + p) * wn
            at_r = (to * pairs + p) * wr
            q_send[p, to, :, 0:wn] = qn[:, at_n : at_n + wn]
            q_send[p, to, :, wn : wn + wr] = qr[:, at_r : at_r + wr]
    if pairs >= 4:
        turn = lax.rem(x + z, 2)
        over_x, over_z = lax.rem(z, 2), 2 + lax.rem(x, 2)
        low, high = 1 - over_x, 5 - over_z
        plan = [
            ("y", low * (1 - turn) + high * turn),
            ("x", over_x),
            ("z", over_z),
            ("y", low * turn + high * (1 - turn)),
        ]
    else:
        plan = [(TRY, 0)]

    pl.semaphore_wait(barrier, len(y_peers) + 2 * len(ring))

    fetched = []
    for i, (way, p) in enumerate(plan):
        if way == "y":
            continue
        far = x if way == "x" else z
        fetched.append((i, way, p, far))
        for hop in range(2):
            chip = at(y, 2 * n - far - hop * (n // 2))

            def fetch(dc, p=p, i=i, hop=hop, chip=chip):
                peer = 2 * chip + lax.rem(core + dc, 2)
                pltpu.make_async_remote_copy(
                    src_ref=q_send.at[p, peer],
                    dst_ref=q_recv.at[p, y, core],
                    send_sem=fs_sem.at[i, hop, dc],
                    recv_sem=fr_sem.at[i, hop],
                    device_id=(c, peer),
                    device_id_type=MESH,
                ).start()

            fetch(1)

            @pl.when(far != hop * (n // 2))
            def _(fetch=fetch):
                fetch(0)

            @pl.when(far == hop * (n // 2))
            def _(p=p, i=i, hop=hop):
                pltpu.make_async_copy(q_send.at[p, g], q_recv.at[p, y, core], fr_sem.at[i, hop]).start()

    def send_direct(i, p):
        for d, dc in y_peers:
            peer = 2 * at(y, d) + lax.rem(core + dc, 2)
            pltpu.make_async_remote_copy(
                src_ref=q_send.at[p, peer],
                dst_ref=q_recv.at[p, y, core],
                send_sem=qs_sem.at[i],
                recv_sem=qr_sem.at[i],
                device_id=(c, peer),
                device_id_type=MESH,
            ).start()
        q_recv[p, y, core] = q_send[p, g]

    direct = [(i, p) for i, (way, p) in enumerate(plan) if way == "y"]
    for i, p in direct[:1]:
        send_direct(i, p)

    loads[6].wait()
    loads[7].wait()
    lane = lax.broadcasted_iota(jnp.int32, (1, slots), 1)
    for h in range(n):
        for q in range(2):
            ids = ids_ref[h, q : q + 1, :]
            live = lane < counts_ref[q, h]
            for b in range(keys // BLOCK):
                hit = (ids == c * (keys // BLOCK) + b) & live
                chosen = jnp.max(jnp.where(hit, 0.0, NONE), axis=1, keepdims=True)
                bias[h, q : q + 1, b * BLOCK : (b + 1) * BLOCK] = jnp.broadcast_to(chosen, (1, BLOCK))

    loads[4].wait()
    rkpad[...] = jnp.zeros_like(rkpad)
    rkpad[0, 0:rope] = rk[...]
    rkpad[1, rope : 2 * rope] = rk[...]
    for i, way, p, far in fetched:
        for hop, reach in ((0, near), (1, nearest)):
            chip = at(y, far + hop * (n // 2))
            wait_bytes(q_recv.at[p, chip], fr_sem.at[i, hop])
            for d in reach:
                to = z * n + at(x, d) if way == "x" else at(z, d) * n + x
                pltpu.make_async_remote_copy(
                    src_ref=q_recv.at[p, chip],
                    dst_ref=q_recv.at[p, chip],
                    send_sem=ws_sem.at[i],
                    recv_sem=qr_sem.at[i],
                    device_id=(to, g),
                    device_id_type=MESH,
                ).start()
        if way == "x":
            for j, other in direct[1:]:
                send_direct(j, other)
    loads[2].wait()
    loads[3].wait()
    vext[:, :, vdim:] = jnp.ones((n, keys, vext.shape[2] - vdim), BF16)

    def make_values(h, carry):
        vext[h, :, 0:vdim] = jnp.dot(lat[...], ev[h], preferred_element_type=F32).astype(BF16)
        return carry

    lax.fori_loop(0, n, make_values, 0)
    loads[5].wait()

    scale = 1.0 / math.sqrt(nope + rope)
    row = lax.broadcasted_iota(jnp.int32, (2 * half, 1), 0)
    in_half = lax.rem(row, half)
    token = (2 * (in_half // tok) + row // half) * tok + lax.rem(in_half, tok)
    context = keys * n * n
    query_pos = context - 2 * half + token
    late = keys // 2
    key_pos = c * keys + late + lax.broadcasted_iota(jnp.int32, (1, keys - late), 1)

    def attend(i, carry):
        p = 0
        for j, (way, which) in enumerate(plan):
            p = jnp.where(i == j, which, p)

            @pl.when(i == j)
            def _(way=way, which=which, j=j):
                if way == "y":
                    wait_bytes(q_send.at[which, pl.ds(0, 2 * n - 1)], qr_sem.at[j])
                elif near:
                    wait_bytes(q_recv.at[which, pl.ds(0, n - 2)], qr_sem.at[j])

        queries = jnp.concatenate(
            [q_recv[p, :, e].reshape(half, wn + wr) for e in range(2)], axis=0
        )
        for k in range(2):
            h = 2 * p + k
            query_latent = jnp.dot(
                queries[:, k * nope : (k + 1) * nope], ak[h], preferred_element_type=F32
            ).astype(BF16)
            scores = lax.dot_general(
                query_latent, lat[...], (((1,), (1,)), ((), ())), preferred_element_type=F32
            )
            scores = scores + jnp.dot(
                queries[:, wn : wn + wr], rkpad[k], preferred_element_type=F32
            )
            scores = scores * scale
            low, high = bias[h, 0:1], bias[h, 1:2]
            quarter = (half // 2, keys)
            mask = jnp.concatenate(
                [jnp.broadcast_to(v, quarter) for v in (low, high, low, high)], axis=0
            )
            scores = scores + mask
            scores = jnp.concatenate(
                [
                    scores[:, :late],
                    jnp.where(key_pos <= query_pos, scores[:, late:], NONE),
                ],
                axis=1,
            )
            top = jnp.max(scores, axis=1, keepdims=True)
            weights = jnp.exp(scores - top).astype(BF16)
            summed = jnp.dot(weights, vext[h], preferred_element_type=F32)
            total = summed[:, vdim : 2 * vdim]
            mixed = summed[:, :vdim] / total
            level = top + jnp.log(total)
            for e in range(2):
                part = slice(e * half, (e + 1) * half)
                o1_send[e, h] = mixed[part].astype(BF16)
                l1_send[e, h] = jnp.transpose(level[part, 0:BLOCK])[0:1]
                mine = x if e == 0 else z
                to = z * n + h if e == 0 else h * n + x
                slot = lax.rem(h - mine + n, n) - 1

                @pl.when(h != mine)
                def _(e=e, h=h, to=to, slot=slot):
                    pltpu.make_async_remote_copy(
                        src_ref=o1_send.at[e, h],
                        dst_ref=o1_recv.at[e, slot],
                        send_sem=s1_sem.at[e, 0],
                        recv_sem=r1_sem.at[e, 0],
                        device_id=(to, g),
                        device_id_type=MESH,
                    ).start()
                    pltpu.make_async_remote_copy(
                        src_ref=l1_send.at[e, h],
                        dst_ref=l1_recv.at[e, slot],
                        send_sem=s1_sem.at[e, 1],
                        recv_sem=r1_sem.at[e, 1],
                        device_id=(to, g),
                        device_id_type=MESH,
                    ).start()

        return carry

    lax.fori_loop(0, pairs, attend, 0)

    for e in range(2):
        mine = x if e == 0 else z
        wait_bytes(o1_recv.at[e], r1_sem.at[e, 0])
        wait_bytes(l1_recv.at[e], r1_sem.at[e, 1])
        levels = jnp.concatenate(
            [l1_send[e, mine]] + [l1_recv[e, k] for k in range(n - 1)], axis=0
        )
        top = jnp.max(levels, axis=0, keepdims=True)
        share = jnp.exp(levels - top)
        whole = jnp.sum(share, axis=0, keepdims=True)
        columns = jnp.transpose(share / whole)
        mixed = columns[:, 0:1] * o1_send[e, mine].astype(F32)
        for k in range(n - 1):
            mixed = mixed + columns[:, k + 1 : k + 2] * o1_recv[e, k].astype(F32)
        o2_send[e] = mixed.astype(BF16)
        l2_send[e] = top + jnp.log(whole)
        for d in ring:
            other = at(z, d) if e == 0 else at(x, d)
            to = other * n + x if e == 0 else z * n + other
            rows = pl.ds(pl.multiple_of(other * tok, tok), tok)
            pltpu.make_async_remote_copy(
                src_ref=o2_send.at[e, rows],
                dst_ref=o2_recv.at[e, d - 1],
                send_sem=s2_sem.at[e, 0],
                recv_sem=r2_sem.at[e, 0],
                device_id=(to, g),
                device_id_type=MESH,
            ).start()
            pltpu.make_async_remote_copy(
                src_ref=l2_send.at[e],
                dst_ref=l2_recv.at[e, d - 1],
                send_sem=s2_sem.at[e, 1],
                recv_sem=r2_sem.at[e, 1],
                device_id=(to, g),
                device_id_type=MESH,
            ).start()

    selves = []
    for e in range(2):
        pos = z if e == 0 else x
        wait_bytes(o2_recv.at[e], r2_sem.at[e, 0])
        wait_bytes(l2_recv.at[e], r2_sem.at[e, 1])
        rows = pl.ds(pl.multiple_of(pos * tok, tok), tok)
        levels = jnp.concatenate([l2_send[e]] + [l2_recv[e, k] for k in range(n - 1)], axis=0)
        share = jnp.exp(levels - jnp.max(levels, axis=0, keepdims=True))
        shares[e] = jnp.transpose(share / jnp.sum(share, axis=0, keepdims=True))
        columns = shares[e, rows]
        mixed = columns[:, 0:1] * o2_send[e, rows].astype(F32)
        for k in range(n - 1):
            mixed = mixed + columns[:, k + 1 : k + 2] * o2_recv[e, k].astype(F32)
        done[e] = mixed.astype(BF16)
        place = x if e == 0 else z
        peer = 2 * pos + e
        is_self = g == peer
        step = lax.rem(y - pos + n, n)
        selves.append(is_self)
        for hop, shift in enumerate((0, n // 2)):
            for d in [0] * hop + ring:
                to = at(z, d) * n + at(x, shift) if e == 0 else at(z, shift) * n + at(x, d)
                pltpu.make_async_remote_copy(
                    src_ref=done.at[e],
                    dst_ref=rows_all.at[place, g],
                    send_sem=s3_sem.at[e],
                    recv_sem=r3_sem.at[hop, step],
                    device_id=(to, peer),
                    device_id_type=MESH,
                ).start()

        @pl.when(is_self)
        def _(e=e, place=place):
            pltpu.make_async_copy(done.at[e], rows_all.at[place, g], r3_sem.at[0, 0]).start()

        @pl.when(jnp.logical_not(is_self))
        def _(e=e, place=place, peer=peer):
            pltpu.make_async_remote_copy(
                src_ref=done.at[e],
                dst_ref=rows_all.at[place, g],
                send_sem=s3_sem.at[e],
                recv_sem=r3_sem.at[0, step],
                device_id=(c, peer),
                device_id_type=MESH,
            ).start()

    place = x * (1 - core) + z * core
    for hop, reach in ((0, near), (1, nearest)):
        held = at(place, hop * (n // 2))
        for step in [0] + ring:
            both = rows_all.at[held, pl.ds(2 * at(y, step), 2)]
            wait_bytes(both, r3_sem.at[hop, step])
            for d in reach:
                to = (z * n + at(x, d)) * (1 - core) + (at(z, d) * n + x) * core
                pltpu.make_async_remote_copy(
                    src_ref=both,
                    dst_ref=both,
                    send_sem=s4_sem,
                    recv_sem=r4_sem.at[(hop * (n // 2) - d) % n],
                    device_id=(to, g),
                    device_id_type=MESH,
                ).start()
    for off in [0, n // 2] + [d for d in ring if d != n // 2]:
        held = at(place, off)
        if off % (n // 2):
            wait_bytes(rows_all.at[held], r4_sem.at[off])
        for group in range(2 * n):
            col = pl.multiple_of((group * n + held) * vdim, vdim)
            out_ref[:, pl.ds(col, vdim)] = rows_all[held, group]

    for i, (way, p) in enumerate(plan):
        if way == "y":
            wait_bytes(q_send.at[p, pl.ds(0, 2 * n - 1)], qs_sem.at[i])
            continue
        for hop in range(2):
            wait_bytes(q_send.at[p, 0], fs_sem.at[i, hop, 1])

            @pl.when((x if way == "x" else z) != hop * (n // 2))
            def _(p=p, i=i, hop=hop):
                wait_bytes(q_send.at[p, 0], fs_sem.at[i, hop, 0])

        if near:
            wait_bytes(q_recv.at[p, pl.ds(0, n - 2)], ws_sem.at[i])
    for e in range(2):
        wait_bytes(o1_recv.at[e], s1_sem.at[e, 0])
        wait_bytes(l1_recv.at[e], s1_sem.at[e, 1])
        wait_bytes(o2_recv.at[e], s2_sem.at[e, 0])
        wait_bytes(l2_recv.at[e], s2_sem.at[e, 1])

        @pl.when(selves[e])
        def _(e=e):
            wait_bytes(rows_all.at[0, pl.ds(0, 2 * n - 1)], s3_sem.at[e])

        @pl.when(jnp.logical_not(selves[e]))
        def _(e=e):
            wait_bytes(rows_all.at[0], s3_sem.at[e])

    if near:
        wait_bytes(rows_all.at[pl.ds(0, len(near) + len(nearest))], s4_sem)


def body(n, qn, qr, lat, rk, ak, ev, ids, counts):
    tok = qn.shape[0]
    half = n * tok
    nope, rope = ak.shape[1], rk.shape[0]
    keys, latent = lat.shape
    vdim = ev.shape[2]
    pairs = n // 2
    vmem = pltpu.VMEM
    dma = pltpu.SemaphoreType.DMA
    return pl.pallas_call(
        functools.partial(kernel, n),
        out_shape=pltpu.VMEM((tok, 2 * n * n * vdim), BF16),
        in_specs=[pl.BlockSpec(memory_space=pltpu.HBM)] * 8,
        out_specs=pl.BlockSpec(memory_space=pltpu.VMEM),
        scratch_shapes=[
            vmem(qn.shape, BF16),
            vmem(qr.shape, BF16),
            vmem(lat.shape, BF16),
            vmem(rk.shape, BF16),
            vmem(ak.shape, BF16),
            vmem(ev.shape, BF16),
            vmem(ids.shape, jnp.int32),
            pltpu.SMEM(counts.shape[::-1], jnp.int32),
            vmem((2, 2 * rope, keys), BF16),
            vmem((n, keys, 2 * vdim), BF16),
            vmem((n, 2, keys), F32),
            vmem((pairs, 2 * n, tok, 2 * (nope + rope)), BF16),
            vmem((pairs, n, 2, tok, 2 * (nope + rope)), BF16),
            vmem((2, n, half, vdim), BF16),
            vmem((2, n, 1, half), F32),
            vmem((2, n - 1, half, vdim), BF16),
            vmem((2, n - 1, 1, half), F32),
            vmem((2, half, vdim), BF16),
            vmem((2, 1, half), F32),
            vmem((2, n - 1, tok, vdim), BF16),
            vmem((2, n - 1, 1, half), F32),
            vmem((2, half, n), F32),
            vmem((2, tok, vdim), BF16),
            vmem((n, 2 * n, tok, vdim), BF16),
            dma((8,)),
            dma((pairs,)),
            dma((pairs,)),
            dma((pairs, 2, 2)),
            dma((pairs, 2)),
            dma((pairs,)),
            dma((2, 2)),
            dma((2, 2)),
            dma((2, 2)),
            dma((2, 2)),
            dma((2,)),
            dma((2, n)),
            dma,
            dma((n,)),
        ],
        compiler_params=pltpu.CompilerParams(
            collective_id=0, has_side_effects=True, vmem_limit_bytes=60 * 1024 * 1024
        ),
        cost_estimate=pl.CostEstimate(
            flops=3 * 10**9, bytes_accessed=4 * 10**6, transcendentals=10**6
        ),
    )(qn, qr, lat, rk, ak, ev, ids, counts.T)


def solution(mesh):
    n = math.isqrt(mesh.shape["ctx"])
    return jax.shard_map(
        functools.partial(body, n),
        mesh=mesh,
        in_specs=(
            P("head", None),
            P("head", None),
            P("ctx", None),
            P(None, "ctx"),
            P("head", None, None),
            P("head", None, None),
            P("head", None, None),
            P("head", None),
        ),
        out_specs=P("head", None),
        check_vma=False,
    )
```
